512 devices in a mesh: grp: 16 (over y, x), node: 32 (over z, core).
Axes of the slice: x: 4, y: 4, z: 16, core: 2. Of those that a mesh axis runs over, the one named last changes fastest.
Arguments:
- damage: bfloat16 [4096, 65536], P('grp', 'node'), may hold values from -6 to 6
- basis_table: bfloat16 [4096, 512], P('grp'), may hold values from -6 to 6
- train_ids: int32 [4096], P('grp'), may hold values from 0 to 4095, each once
- counts: int32 [16], replicated, may hold values from 64 to 256
- new_table: bfloat16 [2048, 512], replicated, may hold values from -6 to 6
- new_ids: int32 [1024], replicated, may hold values from 0 to 2047
Outputs:
- surrogate: bfloat16 [1024, 65536], P('grp', 'node')
- peak: float32 [1024], P('grp')
- spread: float32 [1024], P('grp')
The draws below stay inside these ranges and needn't reach their ends.
Inputs may be any that keep to these rules, and one draw needn't show every extreme that they name: `train_ids`: each row of basis_table is named by exactly one slot.
All inputs are finite; a program needn't handle non-finite values.
Results may differ from the reference program's by a relative error of at most 0.0085.
Values may be sent and summed in bfloat16 or wider, within the bound.
A program may use at most 64 MiB of HBM per device.

```python
import jax
import jax.numpy as jnp
from jax import lax

TERMS = 512
SLOT = 256
NODE_DEV = 2048
GROUPS = 16
SAMPLES = 4096
NODES = 65536
NEW_SAMPLES = 1024
NEW_TABLE_ROWS = 2048
N_NODE = 32


def touch_ends(values, rng, least, largest):
    extent = values.shape
    spot = [jax.random.randint(jax.random.fold_in(rng, axis), (), 0, extent[axis]) for axis in range(len(extent))]
    values = values.at[tuple(spot)].set(least)
    longest = extent.index(max(extent))
    spot[longest] = (spot[longest] + 1) % extent[longest]
    return values.at[tuple(spot)].set(largest)


def block_levels(rng, shape, pieces, least, top_value):
    level, own = 1.0, jax.random.fold_in(rng, 6)
    for position, blocks in pieces:
        draws = jnp.exp(jax.random.uniform(jax.random.fold_in(own, position), (blocks,), jnp.float32, least / len(pieces), top_value / len(pieces)))
        level = level * jnp.repeat(draws, shape[position] // blocks).reshape([-1 if axis == position else 1 for axis in range(len(shape))])
    return level


def centred(rng, extent, scale, limit, cuts=(), kind=jnp.bfloat16):
    loudness = block_levels(rng, extent, cuts, -0.22, 0.18) if cuts else 1.0
    drawn = jax.random.normal(rng, extent, jnp.float32) * scale * loudness
    return jnp.minimum(jnp.maximum(drawn, -limit), limit).astype(kind)


def setup_inputs(seed: int = 0) -> dict:
    key_list = jax.random.split(jax.random.key(seed), 7)
    damage = centred(key_list[0], (SAMPLES, NODES), 1.0, 6.0, ((0, 16), (1, 32)))
    basis_table = centred(key_list[1], (SAMPLES, TERMS), 1.0, 6.0, ((0, 16),))
    train_ids = jax.random.permutation(key_list[2], SAMPLES).astype(jnp.int32)
    counts = touch_ends(jax.random.randint(key_list[3], (GROUPS,), SLOT // 4, SLOT + 1), jax.random.fold_in(key_list[3], 1), SLOT // 4, SLOT).astype(jnp.int32)
    new_table = centred(key_list[4], (NEW_TABLE_ROWS, TERMS), 1.0, 6.0)
    new_ids = touch_ends(jax.random.randint(key_list[5], (NEW_SAMPLES,), 0, NEW_TABLE_ROWS), jax.random.fold_in(key_list[5], 1), 0, NEW_TABLE_ROWS - 1).astype(jnp.int32)
    return {"damage": damage, "basis_table": basis_table, "train_ids": train_ids, "counts": counts, "new_table": new_table, "new_ids": new_ids}


def reference(damage, basis_table, train_ids, counts, new_table, new_ids):
    slot_index = jnp.arange(SAMPLES, dtype=jnp.int32)
    live_slot = slot_index % SLOT < counts[slot_index // SLOT]
    sample_total = jnp.sum(counts).astype(jnp.float32)
    chosen = jnp.take(basis_table, train_ids, axis=0)
    weighted = jnp.where(live_slot[:, None], chosen, jnp.zeros_like(chosen)).astype(jnp.float32)
    new_rows = jnp.take(new_table, new_ids, axis=0).astype(jnp.float32)

    def one_block(block_index):
        offset = (block_index * NODE_DEV).astype(jnp.int32)
        block_data = lax.dynamic_slice_in_dim(damage, offset, NODE_DEV, 1).astype(jnp.float32)
        coef_full = jnp.dot(weighted.T, block_data, precision=lax.Precision.HIGHEST) / sample_total
        coef_half = lax.optimization_barrier(coef_full.astype(jnp.bfloat16)).astype(jnp.float32)
        values = jnp.dot(new_rows, coef_half, precision=lax.Precision.HIGHEST)
        return (values.astype(jnp.bfloat16), lax.optimization_barrier(jnp.max(values, axis=1)), lax.optimization_barrier(jnp.sum(values * values, axis=1)))
    fields, peaks, squares = lax.map(one_block, jnp.arange(N_NODE, dtype=jnp.int32))
    surrogate = jnp.transpose(fields, (1, 0, 2)).reshape(NEW_SAMPLES, NODES)
    peak = lax.optimization_barrier(jnp.max(peaks, axis=0))
    spread = jnp.sqrt(lax.optimization_barrier(jnp.sum(squares, axis=0)) / NODES + 1e-06)
    return (surrogate, peak, spread)
```

```python
import functools

import jax
import jax.numpy as jnp
from jax import lax
from jax.experimental import pallas as pl
from jax.experimental.pallas import tpu as pltpu
from jax.sharding import PartitionSpec as P

MESH = pl.DeviceIdType.MESH
F32 = jnp.float32
BF16 = jnp.bfloat16


def side_of(count):
    side = 1
    while side * side < count:
        side *= 2
    return side


def near_first(count):
    order = [0]
    for step in range(1, count // 2 + 1):
        order += [step, -step]
    return order[:count]


def kernel(
    sizes,
    damage_hbm, basis_hbm, ids_ref, counts_ref, table_hbm, new_ids_ref,
    out_ref, peak_ref, spread_ref,
    damage, basis, table, onehot, parts, weights, partial, first_in, half, second_in,
    coef, pick, chosen, sending, field, stat_own, stat_pair, stat_all,
    local_sem, part_send, part_recv, weight_send, weight_recv, twin_send, twin_recv,
    first_send, first_recv, second_send, second_recv, field_send, field_recv,
    stat_send, stat_recv,
):
    groups, nodes, slots, terms, cells, samples, rows = sizes
    edge = side_of(groups)
    depth = nodes // 2
    chunk = terms // nodes
    block = cells // groups
    share = samples // groups
    stages = partial.shape[0]
    per_stage = depth // stages
    lines = per_stage * chunk
    offsets = near_first(depth)

    grp = lax.axis_index("grp")
    node = lax.axis_index("node")
    col, row = lax.rem(grp, edge), lax.div(grp, edge)
    level, core = lax.div(node, 2), lax.rem(node, 2)
    twin = level * 2 + (1 - core)

    def grp_peer(step):
        return lax.rem(grp + step + groups, groups)

    def level_peer(step):
        return lax.rem(level + step + depth, depth) * 2 + core

    def in_row(step):
        return lax.rem(col + step, edge)

    def in_col(step):
        return lax.rem(row + step, edge)

    sent = []

    def send(src, dst, send_sem, recv_sem, to):
        copy = pltpu.make_async_remote_copy(
            src_ref=src, dst_ref=dst, send_sem=send_sem, recv_sem=recv_sem,
            device_id=to, device_id_type=MESH,
        )
        copy.start()
        sent.append(copy)

    def arrived(dst, send_sem, recv_sem):
        pltpu.make_async_remote_copy(
            src_ref=dst, dst_ref=dst, send_sem=send_sem, recv_sem=recv_sem,
            device_id=(grp, twin), device_id_type=MESH,
        ).wait_recv()

    load_basis = pltpu.make_async_copy(basis_hbm, basis, local_sem.at[0])
    load_damage = pltpu.make_async_copy(damage_hbm, damage, local_sem.at[1])
    load_table = pltpu.make_async_copy(table_hbm, table, local_sem.at[2])
    load_basis.start()
    load_damage.start()
    load_table.start()

    barrier = pltpu.get_barrier_semaphore()
    for step in range(1, groups):
        pl.semaphore_signal(barrier, inc=1, device_id=(grp_peer(step), node), device_id_type=MESH)
    for step in range(1, depth):
        pl.semaphore_signal(barrier, inc=1, device_id=(grp, level_peer(step)), device_id_type=MESH)
    pl.semaphore_signal(barrier, inc=1, device_id=(grp, twin), device_id_type=MESH)

    ids = ids_ref[...]
    line = lax.broadcasted_iota(jnp.int32, (slots, slots), 0)
    wanted = jnp.broadcast_to(ids, (slots, slots)) - line

    @pl.loop(0, groups)
    def _(g):
        onehot[g] = jnp.where(wanted == g * slots, 1.0, 0.0).astype(BF16)

    total = jnp.int32(0)
    for g in range(groups):
        total = total + counts_ref[g]
    live = counts_ref[grp]
    total = total.astype(F32)

    load_basis.wait()
    pick_terms = lax.broadcasted_iota(jnp.int32, (chunk, terms), 1) - node * chunk
    pick_terms = pick_terms == lax.broadcasted_iota(jnp.int32, (chunk, terms), 0)
    parts[grp] = lax.dot_general(
        jnp.where(pick_terms, 1.0, 0.0).astype(BF16), basis[...],
        (((1,), (1,)), ((), ())), preferred_element_type=F32,
    ).astype(BF16)

    pl.semaphore_wait(barrier, groups - 1 + depth)

    for step in range(1, groups):
        send(parts.at[grp], parts.at[grp], part_send.at[step], part_recv.at[step], (grp_peer(step), node))

    mine = jnp.dot(parts[grp], onehot[grp], preferred_element_type=F32)
    for step in range(1, groups):
        source = grp_peer(-step)
        arrived(parts.at[source], part_send.at[step], part_recv.at[step])
        mine = mine + jnp.dot(parts[source], onehot[source], preferred_element_type=F32)
    slot = lax.broadcasted_iota(jnp.int32, (chunk, slots), 1)
    weights[0, 0] = jnp.where(slot < live, mine, 0.0).astype(BF16)

    send(weights.at[0, 0], weights.at[0, 1], twin_send.at[0], twin_recv.at[0], (grp, twin))
    for k in range(1, depth):
        send(weights.at[0, 0], weights.at[k, 0], weight_send.at[k], weight_recv.at[k], (grp, level_peer(-offsets[k])))

    def pass_on(stage):
        for k in range(stage * per_stage, (stage + 1) * per_stage):
            if k:
                arrived(weights.at[k, 0], weight_send.at[k], weight_recv.at[k])
                send(weights.at[k, 0], weights.at[k, 1], twin_send.at[k], twin_recv.at[k], (grp, twin))

    def project(stage):
        for k in range(stage * per_stage, (stage + 1) * per_stage):
            arrived(weights.at[k, 1], twin_send.at[k], twin_recv.at[k])
        left = weights[stage * per_stage : (stage + 1) * per_stage].reshape(2 * lines, slots)
        for r in range(edge):
            wide = edge * block
            product = jnp.dot(left, damage[:, r * wide : (r + 1) * wide], preferred_element_type=F32).astype(BF16)
            for c in range(edge):
                piece = product[:, c * block : (c + 1) * block]
                partial[stage, 0, c, r] = piece[:lines]
                partial[stage, 1, r, c] = piece[lines:]
        for step in range(1, edge):
            send(
                partial.at[stage, 0, in_row(step)], first_in.at[stage, 0, step - 1],
                first_send.at[stage, 0, step], first_recv.at[stage, 0, step], (row * edge + in_row(step), node),
            )
            send(
                partial.at[stage, 1, in_col(step)], first_in.at[stage, 1, step - 1],
                first_send.at[stage, 1, step], first_recv.at[stage, 1, step], (in_col(step) * edge + col, node),
            )

    def middle(stage):
        for side, own in ((0, col), (1, row)):
            for step in range(1, edge):
                arrived(first_in.at[stage, side, step - 1], first_send.at[stage, side, step], first_recv.at[stage, side, step])
            for q in range(edge):
                amount = partial[stage, side, own, q].astype(F32)
                for step in range(1, edge):
                    amount = amount + first_in[stage, side, step - 1, q].astype(F32)
                half[stage, side, q] = amount.astype(BF16)
        for step in range(1, edge):
            send(
                half.at[stage, 0, in_col(step)], second_in.at[stage, 0, step - 1],
                second_send.at[stage, 0, step], second_recv.at[stage, 0, step], (in_col(step) * edge + col, node),
            )
            send(
                half.at[stage, 1, in_row(step)], second_in.at[stage, 1, step - 1],
                second_send.at[stage, 1, step], second_recv.at[stage, 1, step], (row * edge + in_row(step), node),
            )

    def finish(stage):
        for side, own in ((0, row), (1, col)):
            for step in range(1, edge):
                arrived(second_in.at[stage, side, step - 1], second_send.at[stage, side, step], second_recv.at[stage, side, step])
            amount = half[stage, side, own].astype(F32)
            for step in range(1, edge):
                amount = amount + second_in[stage, side, step - 1].astype(F32)
            amount = (amount / total).astype(BF16)
            for i in range(per_stage):
                at = side * per_stage + i
                k, other = stage * per_stage + at // 2, at % 2
                owner = lax.rem(level + offsets[k] + depth, depth) * 2 + (1 - core if other else core)
                coef[pl.ds(pl.multiple_of(owner * chunk, chunk), chunk), :] = amount[i * chunk : (i + 1) * chunk]

    def choose(part):
        width = samples // edge
        wanted_row = new_ids_ref[:, part * width : (part + 1) * width].astype(F32)
        wanted_row = jnp.broadcast_to(wanted_row, (128, width)).T
        lane = lax.broadcasted_iota(jnp.int32, (width, 128), 1).astype(F32)
        wanted_row = wanted_row - lane
        for q in range(rows // 128):
            pick[:, q * 128 : (q + 1) * 128] = jnp.where(wanted_row == q * 128.0, 1.0, 0.0).astype(BF16)
        chosen[part * width : (part + 1) * width, :] = jnp.dot(
            pick[...], table[...], preferred_element_type=F32
        ).astype(BF16)

    load_damage.wait()
    pass_on(0)
    project(0)
    load_table.wait()
    parts_done = 0
    for stage in range(stages):
        if stage + 1 < stages:
            pass_on(stage + 1)
            project(stage + 1)
        while parts_done < edge * (stage + 1) // stages:
            choose(parts_done)
            parts_done += 1
        middle(stage)
        if stage:
            finish(stage - 1)
    finish(stages - 1)

    for r in range(edge):
        to_row = in_col(r)
        wide = edge * share
        values = jnp.dot(
            chosen[pl.ds(pl.multiple_of(to_row * wide, wide), wide), :], coef[...], preferred_element_type=F32
        ).astype(BF16)
        sending[r] = values.reshape(edge, share, block)
        for c in range(edge):
            to_col = in_row(c)
            here = pl.ds(pl.multiple_of(grp * block, block), block)
            if r == 0 and c == 0:
                field[:, here] = sending[r, to_col]
            else:
                at = r * edge + c
                send(
                    sending.at[r, to_col], field.at[:, here], field_send.at[at], field_recv.at[at],
                    (to_row * edge + to_col, node),
                )

    squares = jnp.zeros((share, block), F32)
    peak = jnp.full((share, block), -jnp.inf, F32)
    for r in range(edge):
        for c in range(edge):
            source = lax.rem(row + edge - r, edge) * edge + lax.rem(col + edge - c, edge)
            here = pl.ds(pl.multiple_of(source * block, block), block)
            if r or c:
                arrived(field.at[:, here], field_send.at[r * edge + c], field_recv.at[r * edge + c])
            piece = field[:, here].astype(F32)
            squares = squares + piece * piece
            peak = jnp.maximum(peak, piece)
    write = pltpu.make_async_copy(field, out_ref, local_sem.at[3])
    write.start()

    stat_own[0:1, :share] = jnp.sum(squares.T, axis=0, keepdims=True)
    stat_own[1:2, :share] = jnp.max(peak.T, axis=0, keepdims=True)
    send(stat_own, stat_pair, stat_send.at[0], stat_recv.at[0], (grp, twin))
    arrived(stat_pair, stat_send.at[0], stat_recv.at[0])
    stat_all[level, 0:1, :] = stat_own[0:1, :] + stat_pair[0:1, :]
    stat_all[level, 1:2, :] = jnp.maximum(stat_own[1:2, :], stat_pair[1:2, :])
    for step in range(1, depth):
        send(stat_all.at[level], stat_all.at[level], stat_send.at[step], stat_recv.at[step], (grp, level_peer(step)))
    for step in range(1, depth):
        source = lax.rem(level - step + depth, depth)
        arrived(stat_all.at[source], stat_send.at[step], stat_recv.at[step])
    everyone = stat_all[...]
    peak_ref[...] = jnp.max(everyone[:, 1, :share], axis=0)
    spread_ref[...] = jnp.sqrt(jnp.sum(everyone[:, 0, :share], axis=0) / (cells * nodes) + 1e-06)

    write.wait()
    for copy in sent:
        copy.wait_send()


def local(damage, basis_table, train_ids, counts, new_table, new_ids):
    groups, nodes = lax.axis_size("grp"), lax.axis_size("node")
    slots, cells = damage.shape
    rows, terms = new_table.shape
    samples = new_ids.shape[0]
    edge, depth = side_of(groups), nodes // 2
    chunk, block, share = terms // nodes, cells // groups, samples // groups
    stages = min(4, depth)
    lines = depth // stages * chunk
    sizes = (groups, nodes, slots, terms, cells, samples, rows)
    dma = pltpu.SemaphoreType.DMA
    any_space = pl.BlockSpec(memory_space=pl.ANY)
    vmem = pl.BlockSpec(memory_space=pltpu.VMEM)
    return pl.pallas_call(
        functools.partial(kernel, sizes),
        out_shape=(
            jax.ShapeDtypeStruct((share, cells), BF16),
            jax.ShapeDtypeStruct((share,), F32),
            jax.ShapeDtypeStruct((share,), F32),
        ),
        in_specs=[any_space, any_space, vmem, pl.BlockSpec(memory_space=pltpu.SMEM), any_space, vmem],
        out_specs=(any_space, vmem, vmem),
        scratch_shapes=[
            pltpu.VMEM((slots, cells), BF16),
            pltpu.VMEM((slots, terms), BF16),
            pltpu.VMEM((rows, terms), BF16),
            pltpu.VMEM((groups, slots, slots), BF16),
            pltpu.VMEM((groups, chunk, slots), BF16),
            pltpu.VMEM((depth, 2, chunk, slots), BF16),
            pltpu.VMEM((stages, 2, edge, edge, lines, block), BF16),
            pltpu.VMEM((stages, 2, edge - 1, edge, lines, block), BF16),
            pltpu.VMEM((stages, 2, edge, lines, block), BF16),
            pltpu.VMEM((stages, 2, edge - 1, lines, block), BF16),
            pltpu.VMEM((terms, block), BF16),
            pltpu.VMEM((samples // edge, rows), BF16),
            pltpu.VMEM((samples, terms), BF16),
            pltpu.VMEM((edge, edge, share, block), BF16),
            pltpu.VMEM((share, cells), BF16),
            pltpu.VMEM((8, 128), F32),
            pltpu.VMEM((8, 128), F32),
            pltpu.VMEM((depth, 8, 128), F32),
            dma((4,)),
            dma((groups,)), dma((groups,)),
            dma((depth,)), dma((depth,)),
            dma((depth,)), dma((depth,)),
            dma((stages, 2, edge)), dma((stages, 2, edge)),
            dma((stages, 2, edge)), dma((stages, 2, edge)),
            dma((groups,)), dma((groups,)),
            dma((depth,)), dma((depth,)),
        ],
        compiler_params=pltpu.CompilerParams(
            collective_id=0, has_side_effects=True, vmem_limit_bytes=48 * 1024 * 1024
        ),
        name="projection",
    )(damage, basis_table, train_ids.reshape(1, -1), counts, new_table, new_ids.reshape(1, -1))


def solution(mesh):
    placed = (P("grp", "node"), P("grp", None), P("grp"), P(), P(), P())
    return jax.shard_map(
        local,
        mesh=mesh,
        in_specs=placed,
        out_specs=(P("grp", "node"), P("grp"), P("grp")),
        check_vma=False,
    )
```

```python
import functools

import jax
import jax.numpy as jnp
from jax import lax
from jax.experimental import pallas as pl
from jax.experimental.pallas import tpu as pltpu
from jax.sharding import PartitionSpec as P

MESH = pl.DeviceIdType.MESH
F32 = jnp.float32
BF16 = jnp.bfloat16


def side_of(count):
    side = 1
    while side * side < count:
        side *= 2
    return side


def near_first(count):
    order = [0]
    for step in range(1, count // 2 + 1):
        order += [step, -step]
    return order[:count]


def stage_plan(window):
    plan, at = [(0, 1)], 1
    while at < window:
        plan.append((at, min(at + 2, window)))
        at += 2
    return plan


def kernel(
    sizes,
    damage_hbm, basis_hbm, ids_hbm, counts_hbm, table_hbm, new_ids_hbm,
    out_ref, stat_ref,
    damage, basis, ids_ref, counts_ref, table, new_ids_ref,
    onehot, parts, weights, partial, first_in, half, second_in,
    coef, pick, chosen, sending, field, stat_out, stat_in, stat_all,
    local_sem, near_sem, far_sem, part_send, part_recv, weight_send, weight_recv,
    first_send, first_recv, second_send, second_recv, field_send, field_recv,
    stat_send, stat_recv, node_send, node_recv,
):
    groups, nodes, slots, terms, cells, samples, rows, window = sizes
    edge = side_of(groups)
    depth = nodes // 2
    chunk = terms // (2 * window)
    block = cells // groups
    share = samples // groups
    plan = stage_plan(window)
    offsets = near_first(window)
    reach = window // 2

    grp = lax.axis_index("grp")
    node = lax.axis_index("node")
    col, row = lax.rem(grp, edge), lax.div(grp, edge)
    level, core = lax.div(node, 2), lax.rem(node, 2)
    twin = level * 2 + (1 - core)

    def place(steps):
        down, along = steps
        return lax.rem(row + down + edge, edge) * edge + lax.rem(col + along + edge, edge)

    def level_peer(step, other=0):
        side = 1 - core if other else core
        return lax.rem(level + step + depth, depth) * 2 + side

    def hops(steps):
        return sum(min(k, edge - k) for k in steps)

    around = sorted(((d, a) for d in range(edge) for a in range(edge) if d or a), key=hops)
    near = sorted({k for k in range(-reach, reach + 1) if k % depth}, key=abs)
    near = [k for i, k in enumerate(near) if k % depth not in [m % depth for m in near[:i]]]
    beside = [k for k in near if abs(k) == 1]

    sent = []

    def send(src, dst, send_sem, recv_sem, to):
        copy = pltpu.make_async_remote_copy(
            src_ref=src, dst_ref=dst, send_sem=send_sem, recv_sem=recv_sem,
            device_id=to, device_id_type=MESH,
        )
        copy.start()
        sent.append(copy)

    def arrived(dst, send_sem, recv_sem):
        pltpu.make_async_remote_copy(
            src_ref=dst, dst_ref=dst, send_sem=send_sem, recv_sem=recv_sem,
            device_id=(grp, twin), device_id_type=MESH,
        ).wait_recv()

    loads = [
        pltpu.make_async_copy(src, dst, local_sem.at[i])
        for i, (src, dst) in enumerate((
            (basis_hbm, basis), (ids_hbm, ids_ref), (counts_hbm, counts_ref), (damage_hbm, damage),
            (table_hbm, table), (new_ids_hbm, new_ids_ref),
        ))
    ]
    loads[0].start()

    barrier = pltpu.get_barrier_semaphore()
    greeted = [(place(steps), node) for steps in reversed(around)]
    greeted += [(grp, level_peer(k)) for k in reversed(near)]
    greeted += [(grp, level_peer(k, 1)) for k in beside] + [(grp, twin)]
    for to in greeted:
        pl.semaphore_signal(barrier, inc=1, device_id=to, device_id_type=MESH)
    for load in loads[1:]:
        load.start()

    index = lax.rem(level, window) * 2 + core
    pick_terms = lax.broadcasted_iota(jnp.int32, (chunk, terms), 1) - index * chunk
    pick_terms = pick_terms == lax.broadcasted_iota(jnp.int32, (chunk, terms), 0)
    pick_terms = jnp.where(pick_terms, 1.0, 0.0).astype(BF16)
    loads[0].wait()
    parts[grp] = lax.dot_general(
        pick_terms, basis[...], (((1,), (1,)), ((), ())), preferred_element_type=F32
    ).astype(BF16)

    pl.semaphore_wait(barrier, len(greeted))

    for steps in reversed(around):
        at = steps[0] * edge + steps[1]
        send(parts.at[grp], parts.at[grp], part_send.at[at], part_recv.at[at], (place(steps), node))
    if depth > window:
        for k in (reach, -reach):
            pl.semaphore_signal(near_sem, inc=1, device_id=(grp, level_peer(k)), device_id_type=MESH)

    loads[1].wait()
    loads[2].wait()
    line = lax.broadcasted_iota(jnp.int32, (slots, slots), 0)
    wanted = jnp.broadcast_to(ids_ref[...], (slots, slots)) - line

    @pl.loop(0, groups)
    def _(g):
        onehot[g] = jnp.where(wanted == g * slots, 1.0, 0.0).astype(BF16)

    counts = counts_ref[...]
    total = jnp.sum(counts, axis=1, keepdims=True).astype(F32)
    which = lax.broadcasted_iota(jnp.int32, counts.shape, 1)
    live = jnp.sum(jnp.where(which == grp, counts, 0), axis=1, keepdims=True)

    mine = jnp.dot(parts[grp], onehot[grp], preferred_element_type=F32)
    for steps in around:
        source = place((-steps[0], -steps[1]))
        at = steps[0] * edge + steps[1]
        arrived(parts.at[source], part_send.at[at], part_recv.at[at])
        mine = mine + jnp.dot(parts[source], onehot[source], preferred_element_type=F32)
    slot = lax.broadcasted_iota(jnp.int32, (chunk, slots), 1)
    weights[0, 0] = jnp.where(slot < live, mine, 0.0).astype(BF16)

    send(weights.at[0, 0], weights.at[0, 1], weight_send.at[0, 1], weight_recv.at[0, 1], (grp, twin))
    for k in range(1, window):
        send(
            weights.at[0, 0], weights.at[k, 0], weight_send.at[k, 0], weight_recv.at[k, 0],
            (grp, level_peer(-offsets[k])),
        )
        if abs(offsets[k]) == 1:
            send(
                weights.at[0, 0], weights.at[k, 1], weight_send.at[k, 1], weight_recv.at[k, 1],
                (grp, level_peer(-offsets[k], 1)),
            )

    def pass_on(stage):
        for k in range(*plan[stage]):
            if k:
                arrived(weights.at[k, 0], weight_send.at[k, 0], weight_recv.at[k, 0])
                if abs(offsets[k]) > 1:
                    send(weights.at[k, 0], weights.at[k, 1], weight_send.at[k, 1], weight_recv.at[k, 1], (grp, twin))

    def lines_of(stage):
        return (plan[stage][1] - plan[stage][0]) * chunk

    def project(stage):
        begin, end = plan[stage]
        lines = lines_of(stage)
        for k in range(begin, end):
            arrived(weights.at[k, 1], weight_send.at[k, 1], weight_recv.at[k, 1])
        left = weights[begin:end].reshape(2 * lines, slots)
        for r in range(edge):
            wide = edge * block
            product = jnp.dot(left, damage[:, r * wide : (r + 1) * wide], preferred_element_type=F32).astype(BF16)
            for c in range(edge):
                piece = product[:, c * block : (c + 1) * block]
                partial[stage, 0, c, r, :lines] = piece[:lines]
                partial[stage, 1, r, c, :lines] = piece[lines:]
        for step in sorted(range(1, edge), key=lambda k: -min(k, edge - k)):
            for side, to in ((0, (0, step)), (1, (step, 0))):
                target = lax.rem((row if side else col) + step, edge)
                send(
                    partial.at[stage, side, target, :, :lines], first_in.at[stage, side, step - 1, :, :lines],
                    first_send.at[stage, side, step], first_recv.at[stage, side, step], (place(to), node),
                )

    def middle(stage):
        lines = lines_of(stage)
        for side, own in ((0, col), (1, row)):
            for step in range(1, edge):
                arrived(
                    first_in.at[stage, side, step - 1, :, :lines],
                    first_send.at[stage, side, step], first_recv.at[stage, side, step],
                )
            for q in range(edge):
                amount = partial[stage, side, own, q, :lines].astype(F32)
                for step in range(1, edge):
                    amount = amount + first_in[stage, side, step - 1, q, :lines].astype(F32)
                half[stage, side, q, :lines] = amount.astype(BF16)
        for step in sorted(range(1, edge), key=lambda k: -min(k, edge - k)):
            for side, to in ((0, (step, 0)), (1, (0, step))):
                target = lax.rem((col if side else row) + step, edge)
                send(
                    half.at[stage, side, target, :lines], second_in.at[stage, side, step - 1, :lines],
                    second_send.at[stage, side, step], second_recv.at[stage, side, step], (place(to), node),
                )

    def finish(stage):
        lines = lines_of(stage)
        begin = plan[stage][0]
        for side, own in ((0, row), (1, col)):
            for step in range(1, edge):
                arrived(
                    second_in.at[stage, side, step - 1, :lines],
                    second_send.at[stage, side, step], second_recv.at[stage, side, step],
                )
            amount = half[stage, side, own, :lines].astype(F32)
            for step in range(1, edge):
                amount = amount + second_in[stage, side, step - 1, :lines].astype(F32)
            amount = (amount / total).astype(BF16)
            for i in range(lines // chunk):
                at = side * (lines // chunk) + i
                k, other = begin + at // 2, at % 2
                owner = lax.rem(level + offsets[k] + depth, window) * 2 + (1 - core if other else core)
                coef[pl.ds(pl.multiple_of(owner * chunk, chunk), chunk), :] = amount[i * chunk : (i + 1) * chunk]

    def choose(part):
        width = samples // edge
        wanted_row = new_ids_ref[:, part * width : (part + 1) * width].astype(F32)
        wanted_row = jnp.broadcast_to(wanted_row, (128, width)).T
        lane = lax.broadcasted_iota(jnp.int32, (width, 128), 1).astype(F32)
        wanted_row = wanted_row - lane
        for q in range(rows // 128):
            pick[:, q * 128 : (q + 1) * 128] = jnp.where(wanted_row == q * 128.0, 1.0, 0.0).astype(BF16)
        chosen[part * width : (part + 1) * width, :] = jnp.dot(
            pick[...], table[...], preferred_element_type=F32
        ).astype(BF16)

    stages = len(plan)
    loads[3].wait()
    project(0)
    pass_on(1)
    loads[4].wait()
    loads[5].wait()
    parts_done = 0
    for stage in range(stages):
        if stage + 1 < stages:
            project(stage + 1)
            if stage + 2 < stages:
                pass_on(stage + 2)
        if parts_done < edge:
            choose(parts_done)
            parts_done += 1
        middle(stage)
        if stage:
            finish(stage - 1)
    while parts_done < edge:
        choose(parts_done)
        parts_done += 1
    if depth > window:
        pl.semaphore_wait(near_sem, 2)
    pl.semaphore_signal(far_sem, inc=1, device_id=(grp, twin), device_id_type=MESH)
    pl.semaphore_wait(far_sem, 1)
    finish(stages - 1)

    def own_stat(values):
        turned = values.T
        return jnp.sum(turned * turned, axis=0, keepdims=True), jnp.max(turned, axis=0, keepdims=True)

    here = pl.ds(pl.multiple_of(grp * block, block), block)
    wide = edge * share
    order = sorted(range(edge), key=lambda k: -min(k, edge - k))
    for r in order:
        to_row = lax.rem(row + r, edge)
        values = jnp.dot(
            chosen[pl.ds(pl.multiple_of(to_row * wide, wide), wide), :], coef[...], preferred_element_type=F32
        )
        square, largest = own_stat(values)
        stat_out[r, 0:1, :] = square
        stat_out[r, 1:2, :] = largest
        sending[r] = values.astype(BF16).reshape(edge, share, block)
        for c in order:
            if r or c:
                at = r * edge + c
                send(stat_out.at[r], stat_in.at[at], stat_send.at[at], stat_recv.at[at], (place((r, c)), node))
    for r in order:
        for c in order:
            to_col = lax.rem(col + c, edge)
            at = r * edge + c
            if at:
                send(sending.at[r, to_col], field.at[:, here], field_send.at[at], field_recv.at[at], (place((r, c)), node))
    field[:, here] = sending[0, col]

    square, largest = stat_out[0, 0:1, :], stat_out[0, 1:2, :]
    for steps in around:
        at = steps[0] * edge + steps[1]
        arrived(stat_in.at[at], stat_send.at[at], stat_recv.at[at])
        square = square + stat_in[at, 0:1, :]
        largest = jnp.maximum(largest, stat_in[at, 1:2, :])
    stat_all[node, 0:1, :] = square
    stat_all[node, 1:2, :] = largest
    for step in sorted(range(depth), key=lambda k: -min(k, depth - k)):
        for other in (0, 1):
            if step or other:
                at = step * 2 + other
                send(
                    stat_all.at[node], stat_all.at[node], node_send.at[at], node_recv.at[at],
                    (grp, level_peer(step, other)),
                )

    for steps in around:
        at = steps[0] * edge + steps[1]
        source = place((-steps[0], -steps[1]))
        there = pl.ds(pl.multiple_of(source * block, block), block)
        arrived(field.at[:, there], field_send.at[at], field_recv.at[at])
    write = pltpu.make_async_copy(field, out_ref, local_sem.at[len(loads)])
    write.start()

    for step in sorted(range(depth), key=lambda k: min(k, depth - k)):
        for other in (0, 1):
            if step or other:
                at = step * 2 + other
                source = level_peer(-step, other)
                arrived(stat_all.at[source], node_send.at[at], node_recv.at[at])
    square, largest = stat_all[0, 0:1, :], stat_all[0, 1:2, :]
    for k in range(1, nodes):
        square = square + stat_all[k, 0:1, :]
        largest = jnp.maximum(largest, stat_all[k, 1:2, :])
    stat_ref[0:1, :] = largest
    stat_ref[1:2, :] = jnp.sqrt(square / (cells * nodes) + 1e-06)

    write.wait()
    for copy in sent:
        copy.wait_send()


def local(damage, basis_table, train_ids, counts, new_table, new_ids):
    groups, nodes = lax.axis_size("grp"), lax.axis_size("node")
    slots, cells = damage.shape
    rows, terms = new_table.shape
    samples = new_ids.shape[0]
    edge, depth = side_of(groups), nodes // 2
    window = min(8, depth)
    chunk, block, share = terms // (2 * window), cells // groups, samples // groups
    stages = len(stage_plan(window))
    lines = 2 * chunk
    sizes = (groups, nodes, slots, terms, cells, samples, rows, window)
    dma = pltpu.SemaphoreType.DMA
    hbm = pl.BlockSpec(memory_space=pl.ANY)
    out, stat = pl.pallas_call(
        functools.partial(kernel, sizes),
        out_shape=(
            jax.ShapeDtypeStruct((share, cells), BF16),
            jax.ShapeDtypeStruct((2, edge * share), F32),
        ),
        in_specs=[hbm] * 6,
        out_specs=(pl.BlockSpec(memory_space=pl.ANY), pl.BlockSpec(memory_space=pltpu.VMEM)),
        scratch_shapes=[
            pltpu.VMEM((slots, cells), BF16),
            pltpu.VMEM((slots, terms), BF16),
            pltpu.VMEM((1, slots), jnp.int32),
            pltpu.VMEM((1, groups), jnp.int32),
            pltpu.VMEM((rows, terms), BF16),
            pltpu.VMEM((1, samples), jnp.int32),
            pltpu.VMEM((groups, slots, slots), BF16),
            pltpu.VMEM((groups, chunk, slots), BF16),
            pltpu.VMEM((window, 2, chunk, slots), BF16),
            pltpu.VMEM((stages, 2, edge, edge, lines, block), BF16),
            pltpu.VMEM((stages, 2, edge - 1, edge, lines, block), BF16),
            pltpu.VMEM((stages, 2, edge, lines, block), BF16),
            pltpu.VMEM((stages, 2, edge - 1, lines, block), BF16),
            pltpu.VMEM((terms, block), BF16),
            pltpu.VMEM((samples // edge, rows), BF16),
            pltpu.VMEM((samples, terms), BF16),
            pltpu.VMEM((edge, edge, share, block), BF16),
            pltpu.VMEM((share, cells), BF16),
            pltpu.VMEM((edge, 2, edge * share), F32),
            pltpu.VMEM((groups, 2, edge * share), F32),
            pltpu.VMEM((nodes, 2, edge * share), F32),
            dma((7,)),
            pltpu.SemaphoreType.REGULAR,
            pltpu.SemaphoreType.REGULAR,
            dma((groups,)), dma((groups,)),
            dma((window, 2)), dma((window, 2)),
            dma((stages, 2, edge)), dma((stages, 2, edge)),
            dma((stages, 2, edge)), dma((stages, 2, edge)),
            dma((groups,)), dma((groups,)),
            dma((groups,)), dma((groups,)),
            dma((nodes,)), dma((nodes,)),
        ],
        compiler_params=pltpu.CompilerParams(
            collective_id=0, has_side_effects=True, vmem_limit_bytes=61950 * 1024
        ),
        name="projection",
    )(damage, basis_table, train_ids.reshape(1, -1), counts.reshape(1, -1), new_table, new_ids.reshape(1, -1))
    at = lax.rem(lax.axis_index("grp"), edge) * share
    stat = lax.dynamic_slice_in_dim(stat, at, share, 1)
    return out, stat[0], stat[1]


def solution(mesh):
    placed = (P("grp", "node"), P("grp", None), P("grp"), P(), P(), P())
    return jax.shard_map(
        local,
        mesh=mesh,
        in_specs=placed,
        out_specs=(P("grp", "node"), P("grp"), P("grp")),
        check_vma=False,
    )
```

```python
import functools

import jax
import jax.numpy as jnp
from jax import lax
from jax.experimental import pallas as pl
from jax.experimental.pallas import tpu as pltpu
from jax.sharding import PartitionSpec as P

MESH = pl.DeviceIdType.MESH
F32 = jnp.float32
BF16 = jnp.bfloat16


def side_of(count):
    side = 1
    while side * side < count:
        side *= 2
    return side


def near_first(count):
    order = [0]
    for step in range(1, count // 2 + 1):
        order += [step, -step]
    return order[:count]


def stage_plan(window):
    cuts = sorted({min(k, window) for k in (0, 1, 3, 7, 11, 15, window)})
    return list(zip(cuts[:-1], cuts[1:]))


def kernel(
    sizes,
    damage_hbm, basis_hbm, ids_hbm, counts_hbm, table_hbm, new_ids_hbm,
    out_ref, stat_ref,
    damage, basis, ids_ref, counts_ref, table, new_ids_ref,
    onehot, parts, weights, partial, first_in, half, second_in,
    coef, pick, chosen, sending, field, stat_out, stat_in, stat_all,
    local_sem, near_sem, far_sem, part_send, part_recv, weight_send, weight_recv,
    first_send, first_recv, second_send, second_recv, field_send, field_recv,
    stat_send, stat_recv, node_send, node_recv,
):
    groups, nodes, slots, terms, cells, samples, rows, window = sizes
    edge = side_of(groups)
    depth = nodes // 2
    chunk = terms // (2 * window)
    block = cells // groups
    share = samples // groups
    plan = stage_plan(window)
    offsets = near_first(window)
    reach = min(4, depth // 2)
    relayed = depth > 2 * reach

    grp = lax.axis_index("grp")
    node = lax.axis_index("node")
    col, row = lax.rem(grp, edge), lax.div(grp, edge)
    level, core = lax.div(node, 2), lax.rem(node, 2)
    twin = level * 2 + (1 - core)

    def place(steps):
        down, along = steps
        return lax.rem(row + down + edge, edge) * edge + lax.rem(col + along + edge, edge)

    def level_peer(step, other=0):
        side = 1 - core if other else core
        return lax.rem(level + step + depth, depth) * 2 + side

    def hops(steps):
        return sum(min(k, edge - k) for k in steps)

    around = sorted(((d, a) for d in range(edge) for a in range(edge) if d or a), key=hops)
    near = sorted({k for k in range(-reach, reach + 1) if k % depth}, key=abs)
    near = [k for i, k in enumerate(near) if k % depth not in [m % depth for m in near[:i]]]
    beside = [k for k in near if abs(k) == 1]

    sent = []

    def send(src, dst, send_sem, recv_sem, to):
        copy = pltpu.make_async_remote_copy(
            src_ref=src, dst_ref=dst, send_sem=send_sem, recv_sem=recv_sem,
            device_id=to, device_id_type=MESH,
        )
        copy.start()
        sent.append(copy)

    def arrived(dst, send_sem, recv_sem):
        pltpu.make_async_remote_copy(
            src_ref=dst, dst_ref=dst, send_sem=send_sem, recv_sem=recv_sem,
            device_id=(grp, twin), device_id_type=MESH,
        ).wait_recv()

    loads = [
        pltpu.make_async_copy(src, dst, local_sem.at[i])
        for i, (src, dst) in enumerate((
            (basis_hbm, basis), (ids_hbm, ids_ref), (counts_hbm, counts_ref), (damage_hbm, damage),
            (table_hbm, table), (new_ids_hbm, new_ids_ref),
        ))
    ]
    loads[0].start()

    barrier = pltpu.get_barrier_semaphore()
    greeted = [(place(steps), node) for steps in reversed(around)]
    greeted += [(grp, level_peer(k)) for k in reversed(near)]
    greeted += [(grp, level_peer(k, 1)) for k in beside] + [(grp, twin)]
    for to in greeted:
        pl.semaphore_signal(barrier, inc=1, device_id=to, device_id_type=MESH)
    for load in loads[1:]:
        load.start()

    index = lax.rem(level, window) * 2 + core
    pick_terms = lax.broadcasted_iota(jnp.int32, (chunk, terms), 1) - index * chunk
    pick_terms = pick_terms == lax.broadcasted_iota(jnp.int32, (chunk, terms), 0)
    pick_terms = jnp.where(pick_terms, 1.0, 0.0).astype(BF16)
    loads[0].wait()
    parts[grp] = lax.dot_general(
        pick_terms, basis[...], (((1,), (1,)), ((), ())), preferred_element_type=F32
    ).astype(BF16)

    pl.semaphore_wait(barrier, len(greeted))

    for steps in reversed(around):
        at = steps[0] * edge + steps[1]
        send(parts.at[grp], parts.at[grp], part_send.at[at], part_recv.at[at], (place(steps), node))
    if relayed:
        for k in (reach, -reach):
            pl.semaphore_signal(near_sem, inc=1, device_id=(grp, level_peer(k)), device_id_type=MESH)

    loads[1].wait()
    loads[2].wait()
    line = lax.broadcasted_iota(jnp.int32, (slots, slots), 0)
    wanted = jnp.broadcast_to(ids_ref[...], (slots, slots)) - line

    @pl.loop(0, groups)
    def _(g):
        onehot[g] = jnp.where(wanted == g * slots, 1.0, 0.0).astype(BF16)

    def choose(part):
        width = samples // edge
        wanted_row = new_ids_ref[:, part * width : (part + 1) * width].astype(F32)
        wanted_row = jnp.broadcast_to(wanted_row, (128, width)).T
        lane = lax.broadcasted_iota(jnp.int32, (width, 128), 1).astype(F32)
        wanted_row = wanted_row - lane
        for q in range(rows // 128):
            pick[:, q * 128 : (q + 1) * 128] = jnp.where(wanted_row == q * 128.0, 1.0, 0.0).astype(BF16)
        chosen[part * width : (part + 1) * width, :] = jnp.dot(
            pick[...], table[...], preferred_element_type=F32
        ).astype(BF16)

    loads[4].wait()
    loads[5].wait()
    for part in range(edge // 2):
        choose(part)

    counts = counts_ref[...]
    total = jnp.sum(counts, axis=1, keepdims=True).astype(F32)
    which = lax.broadcasted_iota(jnp.int32, counts.shape, 1)
    live = jnp.sum(jnp.where(which == grp, counts, 0), axis=1, keepdims=True)

    mine = jnp.dot(parts[grp], onehot[grp], preferred_element_type=F32)
    for steps in around:
        source = place((-steps[0], -steps[1]))
        at = steps[0] * edge + steps[1]
        arrived(parts.at[source], part_send.at[at], part_recv.at[at])
        mine = mine + jnp.dot(parts[source], onehot[source], preferred_element_type=F32)
    slot = lax.broadcasted_iota(jnp.int32, (chunk, slots), 1)
    weights[0, 0] = jnp.where(slot < live, mine, 0.0).astype(BF16)

    send(weights.at[0, 0], weights.at[0, 1], weight_send.at[0, 1], weight_recv.at[0, 1], (grp, twin))
    for k in range(1, window):
        if relayed and k == 2 * reach:
            pl.semaphore_wait(near_sem, 2)
        send(
            weights.at[0, 0], weights.at[k, 0], weight_send.at[k, 0], weight_recv.at[k, 0],
            (grp, level_peer(-offsets[k])),
        )
        if abs(offsets[k]) == 1:
            send(
                weights.at[0, 0], weights.at[k, 1], weight_send.at[k, 1], weight_recv.at[k, 1],
                (grp, level_peer(-offsets[k], 1)),
            )

    def pass_on(stage):
        for k in range(*plan[stage]):
            if k:
                arrived(weights.at[k, 0], weight_send.at[k, 0], weight_recv.at[k, 0])
                if abs(offsets[k]) > 1:
                    send(weights.at[k, 0], weights.at[k, 1], weight_send.at[k, 1], weight_recv.at[k, 1], (grp, twin))

    def lines_of(stage):
        return (plan[stage][1] - plan[stage][0]) * chunk

    def project(stage):
        begin, end = plan[stage]
        lines = lines_of(stage)
        for k in range(begin, end):
            arrived(weights.at[k, 1], weight_send.at[k, 1], weight_recv.at[k, 1])
        left = weights[begin:end].reshape(2 * lines, slots)
        for r in range(edge):
            wide = edge * block
            product = jnp.dot(left, damage[:, r * wide : (r + 1) * wide], preferred_element_type=F32).astype(BF16)
            for c in range(edge):
                piece = product[:, c * block : (c + 1) * block]
                partial[stage, 0, c, r, :lines] = piece[:lines]
                partial[stage, 1, r, c, :lines] = piece[lines:]
        for step in sorted(range(1, edge), key=lambda k: -min(k, edge - k)):
            for side, to in ((0, (0, step)), (1, (step, 0))):
                target = lax.rem((row if side else col) + step, edge)
                send(
                    partial.at[stage, side, target, :, :lines], first_in.at[stage, side, step - 1, :, :lines],
                    first_send.at[stage, side, step], first_recv.at[stage, side, step], (place(to), node),
                )

    def middle(stage):
        lines = lines_of(stage)
        for side, own in ((0, col), (1, row)):
            for step in range(1, edge):
                arrived(
                    first_in.at[stage, side, step - 1, :, :lines],
                    first_send.at[stage, side, step], first_recv.at[stage, side, step],
                )
            for q in range(edge):
                amount = partial[stage, side, own, q, :lines].astype(F32)
                for step in range(1, edge):
                    amount = amount + first_in[stage, side, step - 1, q, :lines].astype(F32)
                half[stage, side, q, :lines] = amount.astype(BF16)
        for step in sorted(range(1, edge), key=lambda k: -min(k, edge - k)):
            for side, to in ((0, (step, 0)), (1, (0, step))):
                target = lax.rem((col if side else row) + step, edge)
                send(
                    half.at[stage, side, target, :lines], second_in.at[stage, side, step - 1, :lines],
                    second_send.at[stage, side, step], second_recv.at[stage, side, step], (place(to), node),
                )

    def finish(stage):
        lines = lines_of(stage)
        begin = plan[stage][0]
        for side, own in ((0, row), (1, col)):
            for step in range(1, edge):
                arrived(
                    second_in.at[stage, side, step - 1, :lines],
                    second_send.at[stage, side, step], second_recv.at[stage, side, step],
                )
            amount = half[stage, side, own, :lines].astype(F32)
            for step in range(1, edge):
                amount = amount + second_in[stage, side, step - 1, :lines].astype(F32)
            amount = (amount / total).astype(BF16)
            for i in range(lines // chunk):
                at = side * (lines // chunk) + i
                k, other = begin + at // 2, at % 2
                owner = lax.rem(level + offsets[k] + depth, window) * 2 + (1 - core if other else core)
                coef[pl.ds(pl.multiple_of(owner * chunk, chunk), chunk), :] = amount[i * chunk : (i + 1) * chunk]

    stages = len(plan)
    loads[3].wait()
    project(0)
    pass_on(1)
    parts_done = edge // 2
    for stage in range(stages):
        if stage + 1 < stages:
            project(stage + 1)
            if stage + 2 < stages:
                pass_on(stage + 2)
        if stage and parts_done < edge:
            choose(parts_done)
            parts_done += 1
        middle(stage)
        if stage:
            finish(stage - 1)
    while parts_done < edge:
        choose(parts_done)
        parts_done += 1
    pl.semaphore_signal(far_sem, inc=1, device_id=(grp, twin), device_id_type=MESH)
    pl.semaphore_wait(far_sem, 1)
    finish(stages - 1)

    def own_stat(values):
        turned = values.T
        return jnp.sum(turned * turned, axis=0, keepdims=True), jnp.max(turned, axis=0, keepdims=True)

    here = pl.ds(pl.multiple_of(grp * block, block), block)
    wide = edge * share
    order = sorted(range(edge), key=lambda k: -min(k, edge - k))
    for r in order:
        to_row = lax.rem(row + r, edge)
        values = jnp.dot(
            chosen[pl.ds(pl.multiple_of(to_row * wide, wide), wide), :], coef[...], preferred_element_type=F32
        )
        square, largest = own_stat(values)
        stat_out[r, 0:1, :] = square
        stat_out[r, 1:2, :] = largest
        sending[r] = values.astype(BF16).reshape(edge, share, block)
        for c in order:
            if r or c:
                at = r * edge + c
                send(stat_out.at[r], stat_in.at[at], stat_send.at[at], stat_recv.at[at], (place((r, c)), node))
    for r in order:
        for c in order:
            to_col = lax.rem(col + c, edge)
            at = r * edge + c
            if at:
                send(sending.at[r, to_col], field.at[:, here], field_send.at[at], field_recv.at[at], (place((r, c)), node))
    field[:, here] = sending[0, col]

    square, largest = stat_out[0, 0:1, :], stat_out[0, 1:2, :]
    for steps in around:
        at = steps[0] * edge + steps[1]
        arrived(stat_in.at[at], stat_send.at[at], stat_recv.at[at])
        square = square + stat_in[at, 0:1, :]
        largest = jnp.maximum(largest, stat_in[at, 1:2, :])
    stat_all[node, 0:1, :] = square
    stat_all[node, 1:2, :] = largest
    for step in sorted(range(depth), key=lambda k: -min(k, depth - k)):
        for other in (0, 1):
            if step or other:
                at = step * 2 + other
                send(
                    stat_all.at[node], stat_all.at[node], node_send.at[at], node_recv.at[at],
                    (grp, level_peer(step, other)),
                )

    for steps in around:
        at = steps[0] * edge + steps[1]
        source = place((-steps[0], -steps[1]))
        there = pl.ds(pl.multiple_of(source * block, block), block)
        arrived(field.at[:, there], field_send.at[at], field_recv.at[at])
    write = pltpu.make_async_copy(field, out_ref, local_sem.at[len(loads)])
    write.start()

    for step in sorted(range(depth), key=lambda k: min(k, depth - k)):
        for other in (0, 1):
            if step or other:
                at = step * 2 + other
                source = level_peer(-step, other)
                arrived(stat_all.at[source], node_send.at[at], node_recv.at[at])
    square, largest = stat_all[0, 0:1, :], stat_all[0, 1:2, :]
    for k in range(1, nodes):
        square = square + stat_all[k, 0:1, :]
        largest = jnp.maximum(largest, stat_all[k, 1:2, :])
    spread = jnp.sqrt(square / (cells * nodes) + 1e-06)
    for c in range(edge):
        @pl.when(col == c)
        def _(c=c):
            stat_ref[0:1, :] = largest[:, c * share : (c + 1) * share]
            stat_ref[1:2, :] = spread[:, c * share : (c + 1) * share]

    write.wait()
    for copy in sent:
        copy.wait_send()


def local(damage, basis_table, train_ids, counts, new_table, new_ids):
    groups, nodes = lax.axis_size("grp"), lax.axis_size("node")
    slots, cells = damage.shape
    rows, terms = new_table.shape
    samples = new_ids.shape[0]
    edge, depth = side_of(groups), nodes // 2
    window = depth
    chunk, block, share = terms // (2 * window), cells // groups, samples // groups
    stages = len(stage_plan(window))
    lines = max(end - begin for begin, end in stage_plan(window)) * chunk
    sizes = (groups, nodes, slots, terms, cells, samples, rows, window)
    dma = pltpu.SemaphoreType.DMA
    hbm = pl.BlockSpec(memory_space=pl.ANY)
    out, stat = pl.pallas_call(
        functools.partial(kernel, sizes),
        out_shape=(
            jax.ShapeDtypeStruct((share, cells), BF16),
            jax.ShapeDtypeStruct((2, share), F32),
        ),
        in_specs=[hbm] * 6,
        out_specs=(pl.BlockSpec(memory_space=pl.ANY), pl.BlockSpec(memory_space=pltpu.VMEM)),
        scratch_shapes=[
            pltpu.VMEM((slots, cells), BF16),
            pltpu.VMEM((slots, terms), BF16),
            pltpu.VMEM((1, slots), jnp.int32),
            pltpu.VMEM((1, groups), jnp.int32),
            pltpu.VMEM((rows, terms), BF16),
            pltpu.VMEM((1, samples), jnp.int32),
            pltpu.VMEM((groups, slots, slots), BF16),
            pltpu.VMEM((groups, chunk, slots), BF16),
            pltpu.VMEM((window, 2, chunk, slots), BF16),
            pltpu.VMEM((stages, 2, edge, edge, lines, block), BF16),
            pltpu.VMEM((stages, 2, edge - 1, edge, lines, block), BF16),
            pltpu.VMEM((stages, 2, edge, lines, block), BF16),
            pltpu.VMEM((stages, 2, edge - 1, lines, block), BF16),
            pltpu.VMEM((terms, block), BF16),
            pltpu.VMEM((samples // edge, rows), BF16),
            pltpu.VMEM((samples, terms), BF16),
            pltpu.VMEM((edge, edge, share, block), BF16),
            pltpu.VMEM((share, cells), BF16),
            pltpu.VMEM((edge, 2, edge * share), F32),
            pltpu.VMEM((groups, 2, edge * share), F32),
            pltpu.VMEM((nodes, 2, edge * share), F32),
            dma((7,)),
            pltpu.SemaphoreType.REGULAR,
            pltpu.SemaphoreType.REGULAR,
            dma((groups,)), dma((groups,)),
            dma((window, 2)), dma((window, 2)),
            dma((stages, 2, edge)), dma((stages, 2, edge)),
            dma((stages, 2, edge)), dma((stages, 2, edge)),
            dma((groups,)), dma((groups,)),
            dma((groups,)), dma((groups,)),
            dma((nodes,)), dma((nodes,)),
        ],
        compiler_params=pltpu.CompilerParams(
            collective_id=0, has_side_effects=True, vmem_limit_bytes=61950 * 1024
        ),
        name="projection",
    )(damage, basis_table, train_ids.reshape(1, -1), counts.reshape(1, -1), new_table, new_ids.reshape(1, -1))
    return out, stat[0], stat[1]


def solution(mesh):
    placed = (P("grp", "node"), P("grp", None), P("grp"), P(), P(), P())
    return jax.shard_map(
        local,
        mesh=mesh,
        in_specs=placed,
        out_specs=(P("grp", "node"), P("grp"), P("grp")),
        check_vma=False,
    )
```

```python
import functools

import jax
import jax.numpy as jnp
from jax import lax
from jax.experimental import pallas as pl
from jax.experimental.pallas import tpu as pltpu
from jax.sharding import PartitionSpec as P

MESH = pl.DeviceIdType.MESH
F32 = jnp.float32
BF16 = jnp.bfloat16


def side_of(count):
    side = 1
    while side * side < count:
        side *= 2
    return side


def near_first(count):
    order = [0]
    for step in range(1, count // 2 + 1):
        order += [step, -step]
    return order[:count]


def stage_plan(window):
    cuts = sorted({min(k, 2 * window) for k in (0, 2, 6, 10, 2 * window)})
    return list(zip(cuts[:-1], cuts[1:]))


def kernel(
    sizes,
    damage_hbm, basis_hbm, ids_hbm, counts_hbm, table_hbm, new_ids_hbm,
    out_ref, stat_ref,
    damage, basis, ids_ref, counts_ref, table, new_ids_ref,
    onehot, parts, weights, partial, first_in, half, second_in,
    coef, pick, chosen, sending, field, stat_out, stat_in, stat_all,
    local_sem, relay_sem, far_sem, part_send, part_recv, weight_send, weight_recv,
    first_send, first_recv, second_send, second_recv, field_send, field_recv,
    stat_send, stat_recv, node_send, node_recv,
):
    groups, nodes, slots, terms, cells, samples, rows, window = sizes
    edge = side_of(groups)
    depth = nodes // 2
    chunk = terms // (2 * window)
    block = cells // groups
    share = samples // groups
    plan = stage_plan(window)
    stages = len(plan)
    offsets = near_first(window)
    reach = min(2, depth // 2)
    relays = []
    while (reach << len(relays)) * 2 < depth:
        relays.append(reach << len(relays))

    grp = lax.axis_index("grp")
    node = lax.axis_index("node")
    col, row = lax.rem(grp, edge), lax.div(grp, edge)
    level, core = lax.div(node, 2), lax.rem(node, 2)
    twin = level * 2 + (1 - core)

    def place(steps):
        down, along = steps
        return lax.rem(row + down + edge, edge) * edge + lax.rem(col + along + edge, edge)

    def level_peer(step, other=0):
        side = 1 - core if other else core
        return lax.rem(level + step + depth, depth) * 2 + side

    def hops(steps):
        return sum(min(k, edge - k) for k in steps)

    around = sorted(((d, a) for d in range(edge) for a in range(edge) if d or a), key=hops)
    near = sorted({k for k in range(-reach, reach + 1) if k % depth}, key=abs)
    near = [k for i, k in enumerate(near) if k % depth not in [m % depth for m in near[:i]]]
    beside = [k for k in near if abs(k) == 1]

    sent = []

    def send(src, dst, send_sem, recv_sem, to):
        copy = pltpu.make_async_remote_copy(
            src_ref=src, dst_ref=dst, send_sem=send_sem, recv_sem=recv_sem,
            device_id=to, device_id_type=MESH,
        )
        copy.start()
        sent.append(copy)

    def arrived(dst, send_sem, recv_sem):
        pltpu.make_async_remote_copy(
            src_ref=dst, dst_ref=dst, send_sem=send_sem, recv_sem=recv_sem,
            device_id=(grp, twin), device_id_type=MESH,
        ).wait_recv()

    loads = [
        pltpu.make_async_copy(src, dst, local_sem.at[i])
        for i, (src, dst) in enumerate((
            (basis_hbm, basis), (ids_hbm, ids_ref), (counts_hbm, counts_ref), (damage_hbm, damage),
            (table_hbm, table), (new_ids_hbm, new_ids_ref),
        ))
    ]
    loads[0].start()

    barrier = pltpu.get_barrier_semaphore()
    greeted = [(place(steps), node) for steps in reversed(around)]
    greeted += [(grp, level_peer(k)) for k in reversed(near)]
    greeted += [(grp, level_peer(k, 1)) for k in beside] + [(grp, twin)]
    for to in greeted:
        pl.semaphore_signal(barrier, inc=1, device_id=to, device_id_type=MESH)
    for load in loads[1:]:
        load.start()

    index = lax.rem(level, window) * 2 + core
    pick_terms = lax.broadcasted_iota(jnp.int32, (chunk, terms), 1) - index * chunk
    pick_terms = pick_terms == lax.broadcasted_iota(jnp.int32, (chunk, terms), 0)
    pick_terms = jnp.where(pick_terms, 1.0, 0.0).astype(BF16)
    loads[0].wait()
    parts[grp] = lax.dot_general(
        pick_terms, basis[...], (((1,), (1,)), ((), ())), preferred_element_type=F32
    ).astype(BF16)

    pl.semaphore_wait(barrier, len(greeted))

    for steps in reversed(around):
        at = steps[0] * edge + steps[1]
        send(parts.at[grp], parts.at[grp], part_send.at[at], part_recv.at[at], (place(steps), node))
    def relay(i):
        for k in (relays[i], -relays[i]):
            pl.semaphore_signal(relay_sem.at[i], inc=1, device_id=(grp, level_peer(k)), device_id_type=MESH)

    def hear_relay(i):
        pl.semaphore_wait(relay_sem.at[i], 2)
        if i + 1 < len(relays):
            relay(i + 1)

    if relays:
        relay(0)

    loads[1].wait()
    loads[2].wait()
    line = lax.broadcasted_iota(jnp.int32, (slots, slots), 0)
    wanted = jnp.broadcast_to(ids_ref[...], (slots, slots)) - line

    @pl.loop(0, groups)
    def _(g):
        onehot[g] = jnp.where(wanted == g * slots, 1.0, 0.0).astype(BF16)

    def choose(part):
        width = samples // edge
        wanted_row = new_ids_ref[:, part * width : (part + 1) * width].astype(F32)
        wanted_row = jnp.broadcast_to(wanted_row, (128, width)).T
        lane = lax.broadcasted_iota(jnp.int32, (width, 128), 1).astype(F32)
        wanted_row = wanted_row - lane
        for q in range(rows // 128):
            pick[:, q * 128 : (q + 1) * 128] = jnp.where(wanted_row == q * 128.0, 1.0, 0.0).astype(BF16)
        chosen[part * width : (part + 1) * width, :] = jnp.dot(
            pick[...], table[...], preferred_element_type=F32
        ).astype(BF16)

    loads[4].wait()
    loads[5].wait()
    for part in range(edge):
        choose(part)

    counts = counts_ref[...]
    total = jnp.sum(counts, axis=1, keepdims=True).astype(F32)
    which = lax.broadcasted_iota(jnp.int32, counts.shape, 1)
    live = jnp.sum(jnp.where(which == grp, counts, 0), axis=1, keepdims=True)

    mine = jnp.dot(parts[grp], onehot[grp], preferred_element_type=F32)
    for steps in around:
        source = place((-steps[0], -steps[1]))
        at = steps[0] * edge + steps[1]
        arrived(parts.at[source], part_send.at[at], part_recv.at[at])
        mine = mine + jnp.dot(parts[source], onehot[source], preferred_element_type=F32)
    slot = lax.broadcasted_iota(jnp.int32, (chunk, slots), 1)
    weights[0] = jnp.where(slot < live, mine, 0.0).astype(BF16)

    send(weights.at[0], weights.at[1], weight_send.at[0, 1], weight_recv.at[0, 1], (grp, twin))
    for k in range(1, window):
        if relays and k == 2 * reach + 1:
            hear_relay(0)
        send(
            weights.at[0], weights.at[2 * k], weight_send.at[k, 0], weight_recv.at[k, 0],
            (grp, level_peer(-offsets[k])),
        )
        if abs(offsets[k]) == 1:
            send(
                weights.at[0], weights.at[2 * k + 1], weight_send.at[k, 1], weight_recv.at[k, 1],
                (grp, level_peer(-offsets[k], 1)),
            )

    def pass_on(stage):
        for u in range(*plan[stage]):
            k = u // 2
            if u % 2 == 0 and k:
                arrived(weights.at[2 * k], weight_send.at[k, 0], weight_recv.at[k, 0])
                if abs(offsets[k]) > 1:
                    send(
                        weights.at[2 * k], weights.at[2 * k + 1], weight_send.at[k, 1], weight_recv.at[k, 1],
                        (grp, twin),
                    )

    def lines_of(stage):
        return (plan[stage][1] - plan[stage][0]) * chunk // 2

    def project(stage):
        begin, end = plan[stage]
        lines = lines_of(stage)
        for u in range(begin, end):
            if u % 2:
                arrived(weights.at[u], weight_send.at[u // 2, 1], weight_recv.at[u // 2, 1])
        left = weights[begin:end].reshape(2 * lines, slots)
        for r in range(edge):
            wide = edge * block
            product = jnp.dot(left, damage[:, r * wide : (r + 1) * wide], preferred_element_type=F32).astype(BF16)
            for c in range(edge):
                piece = product[:, c * block : (c + 1) * block]
                partial[stage, 0, c, r, :lines] = piece[:lines]
                partial[stage, 1, r, c, :lines] = piece[lines:]
        for step in sorted(range(1, edge), key=lambda k: -min(k, edge - k)):
            for side, to in ((0, (0, step)), (1, (step, 0))):
                target = lax.rem((row if side else col) + step, edge)
                send(
                    partial.at[stage, side, target, :, :lines], first_in.at[stage, side, step - 1, :, :lines],
                    first_send.at[stage, side, step], first_recv.at[stage, side, step], (place(to), node),
                )

    def middle(stage):
        lines = lines_of(stage)
        for side, own in ((0, col), (1, row)):
            for step in range(1, edge):
                arrived(
                    first_in.at[stage, side, step - 1, :, :lines],
                    first_send.at[stage, side, step], first_recv.at[stage, side, step],
                )
            for q in range(edge):
                amount = partial[stage, side, own, q, :lines].astype(F32)
                for step in range(1, edge):
                    amount = amount + first_in[stage, side, step - 1, q, :lines].astype(F32)
                half[stage, side, q, :lines] = amount.astype(BF16)
        for step in sorted(range(1, edge), key=lambda k: -min(k, edge - k)):
            for side, to in ((0, (step, 0)), (1, (0, step))):
                target = lax.rem((col if side else row) + step, edge)
                send(
                    half.at[stage, side, target, :lines], second_in.at[stage, side, step - 1, :lines],
                    second_send.at[stage, side, step], second_recv.at[stage, side, step], (place(to), node),
                )

    def finish(stage):
        lines = lines_of(stage)
        begin = plan[stage][0]
        for side, own in ((0, row), (1, col)):
            for step in range(1, edge):
                arrived(
                    second_in.at[stage, side, step - 1, :lines],
                    second_send.at[stage, side, step], second_recv.at[stage, side, step],
                )
            amount = half[stage, side, own, :lines].astype(F32)
            for step in range(1, edge):
                amount = amount + second_in[stage, side, step - 1, :lines].astype(F32)
            amount = (amount / total).astype(BF16)
            piece = min(chunk, lines)
            for i in range(lines // piece):
                at = side * lines + i * piece
                u = begin + at // chunk
                owner = lax.rem(level + offsets[u // 2] + depth, window) * 2 + (1 - core if u % 2 else core)
                first = owner * chunk + at % chunk
                coef[pl.ds(pl.multiple_of(first, piece), piece), :] = amount[i * piece : (i + 1) * piece]

    loads[3].wait()
    ahead = min(3, stages)
    for stage in range(ahead):
        pass_on(stage)
        project(stage)
    for stage in range(stages):
        if stage + ahead < stages:
            pass_on(stage + ahead)
        middle(stage)
        if stage + ahead < stages:
            project(stage + ahead)
        if stage:
            finish(stage - 1)
    for i in range(1 if window > 2 * reach + 1 else 0, len(relays)):
        hear_relay(i)
    pl.semaphore_signal(far_sem, inc=1, device_id=(grp, twin), device_id_type=MESH)
    pl.semaphore_wait(far_sem, 1)
    finish(stages - 1)

    def own_stat(values):
        turned = values.T
        return jnp.sum(turned * turned, axis=0, keepdims=True), jnp.max(turned, axis=0, keepdims=True)

    here = pl.ds(pl.multiple_of(grp * block, block), block)
    wide = edge * share
    order = sorted(range(edge), key=lambda k: -min(k, edge - k))
    for r in order:
        to_row = lax.rem(row + r, edge)
        values = jnp.dot(
            chosen[pl.ds(pl.multiple_of(to_row * wide, wide), wide), :], coef[...], preferred_element_type=F32
        )
        square, largest = own_stat(values)
        stat_out[r, 0:1, :] = square
        stat_out[r, 1:2, :] = largest
        sending[r] = values.astype(BF16).reshape(edge, share, block)
        for c in order:
            if r or c:
                at = r * edge + c
                send(stat_out.at[r], stat_in.at[at], stat_send.at[at], stat_recv.at[at], (place((r, c)), node))
    for r in order:
        for c in order:
            to_col = lax.rem(col + c, edge)
            at = r * edge + c
            if at:
                send(sending.at[r, to_col], field.at[:, here], field_send.at[at], field_recv.at[at], (place((r, c)), node))
    field[:, here] = sending[0, col]

    square, largest = stat_out[0, 0:1, :], stat_out[0, 1:2, :]
    for steps in around:
        at = steps[0] * edge + steps[1]
        arrived(stat_in.at[at], stat_send.at[at], stat_recv.at[at])
        square = square + stat_in[at, 0:1, :]
        largest = jnp.maximum(largest, stat_in[at, 1:2, :])
    stat_all[node, 0:1, :] = square
    stat_all[node, 1:2, :] = largest
    for step in sorted(range(depth), key=lambda k: -min(k, depth - k)):
        for other in (0, 1):
            if step or other:
                at = step * 2 + other
                send(
                    stat_all.at[node], stat_all.at[node], node_send.at[at], node_recv.at[at],
                    (grp, level_peer(step, other)),
                )

    for steps in around:
        at = steps[0] * edge + steps[1]
        source = place((-steps[0], -steps[1]))
        there = pl.ds(pl.multiple_of(source * block, block), block)
        arrived(field.at[:, there], field_send.at[at], field_recv.at[at])
    write = pltpu.make_async_copy(field, out_ref, local_sem.at[len(loads)])
    write.start()

    for step in sorted(range(depth), key=lambda k: min(k, depth - k)):
        for other in (0, 1):
            if step or other:
                at = step * 2 + other
                source = level_peer(-step, other)
                arrived(stat_all.at[source], node_send.at[at], node_recv.at[at])
    square, largest = stat_all[0, 0:1, :], stat_all[0, 1:2, :]
    for k in range(1, nodes):
        square = square + stat_all[k, 0:1, :]
        largest = jnp.maximum(largest, stat_all[k, 1:2, :])
    spread = jnp.sqrt(square / (cells * nodes) + 1e-06)
    result = (largest[:, :share], spread[:, :share])
    for c in range(1, edge):
        mine = slice(c * share, (c + 1) * share)
        result = (jnp.where(col == c, largest[:, mine], result[0]), jnp.where(col == c, spread[:, mine], result[1]))
    stat_ref[0:1, :], stat_ref[1:2, :] = result

    write.wait()
    for copy in sent:
        copy.wait_send()


def local(damage, basis_table, train_ids, counts, new_table, new_ids):
    groups, nodes = lax.axis_size("grp"), lax.axis_size("node")
    slots, cells = damage.shape
    rows, terms = new_table.shape
    samples = new_ids.shape[0]
    edge, depth = side_of(groups), nodes // 2
    window = min(8, depth)
    chunk, block, share = terms // (2 * window), cells // groups, samples // groups
    stages = len(stage_plan(window))
    lines = max(end - begin for begin, end in stage_plan(window)) * chunk // 2
    sizes = (groups, nodes, slots, terms, cells, samples, rows, window)
    dma = pltpu.SemaphoreType.DMA
    hbm = pl.BlockSpec(memory_space=pl.ANY)
    out, stat = pl.pallas_call(
        functools.partial(kernel, sizes),
        out_shape=(
            jax.ShapeDtypeStruct((share, cells), BF16),
            jax.ShapeDtypeStruct((2, share), F32),
        ),
        in_specs=[hbm] * 6,
        out_specs=(pl.BlockSpec(memory_space=pl.ANY), pl.BlockSpec(memory_space=pltpu.VMEM)),
        scratch_shapes=[
            pltpu.VMEM((slots, cells), BF16),
            pltpu.VMEM((slots, terms), BF16),
            pltpu.VMEM((1, slots), jnp.int32),
            pltpu.VMEM((1, groups), jnp.int32),
            pltpu.VMEM((rows, terms), BF16),
            pltpu.VMEM((1, samples), jnp.int32),
            pltpu.VMEM((groups, slots, slots), BF16),
            pltpu.VMEM((groups, chunk, slots), BF16),
            pltpu.VMEM((2 * window, chunk, slots), BF16),
            pltpu.VMEM((stages, 2, edge, edge, lines, block), BF16),
            pltpu.VMEM((stages, 2, edge - 1, edge, lines, block), BF16),
            pltpu.VMEM((stages, 2, edge, lines, block), BF16),
            pltpu.VMEM((stages, 2, edge - 1, lines, block), BF16),
            pltpu.VMEM((terms, block), BF16),
            pltpu.VMEM((samples // edge, rows), BF16),
            pltpu.VMEM((samples, terms), BF16),
            pltpu.VMEM((edge, edge, share, block), BF16),
            pltpu.VMEM((share, cells), BF16),
            pltpu.VMEM((edge, 2, edge * share), F32),
            pltpu.VMEM((groups, 2, edge * share), F32),
            pltpu.VMEM((nodes, 2, edge * share), F32),
            dma((7,)),
            pltpu.SemaphoreType.REGULAR((4,)),
            pltpu.SemaphoreType.REGULAR,
            dma((groups,)), dma((groups,)),
            dma((window, 2)), dma((window, 2)),
            dma((stages, 2, edge)), dma((stages, 2, edge)),
            dma((stages, 2, edge)), dma((stages, 2, edge)),
            dma((groups,)), dma((groups,)),
            dma((groups,)), dma((groups,)),
            dma((nodes,)), dma((nodes,)),
        ],
        compiler_params=pltpu.CompilerParams(
            collective_id=0, has_side_effects=True, vmem_limit_bytes=61950 * 1024
        ),
        name="projection",
    )(damage, basis_table, train_ids.reshape(1, -1), counts.reshape(1, -1), new_table, new_ids.reshape(1, -1))
    return out, stat[0], stat[1]


def solution(mesh):
    placed = (P("grp", "node"), P("grp", None), P("grp"), P(), P(), P())
    return jax.shard_map(
        local,
        mesh=mesh,
        in_specs=placed,
        out_specs=(P("grp", "node"), P("grp"), P("grp")),
        check_vma=False,
    )
```

```python
import functools

import jax
import jax.numpy as jnp
from jax import lax
from jax.experimental import pallas as pl
from jax.experimental.pallas import tpu as pltpu
from jax.sharding import PartitionSpec as P

MESH = pl.DeviceIdType.MESH
F32 = jnp.float32
BF16 = jnp.bfloat16


def side_of(count):
    side = 1
    while side * side < count:
        side *= 2
    return side


def near_first(count):
    order = [0]
    for step in range(1, count // 2 + 1):
        order += [step, -step]
    return order[:count]


def stage_plan(window):
    cuts = sorted({min(k, 2 * window) for k in (0, 2, 6, 10, 2 * window)})
    return list(zip(cuts[:-1], cuts[1:]))


def kernel(
    sizes,
    damage_hbm, basis_hbm, ids_hbm, counts_hbm, table_hbm, new_ids_hbm,
    out_ref, stat_ref,
    damage, far_damage, basis, ids_ref, far_ids, counts_ref, table, new_ids_ref,
    onehot, parts, weights, partial, first_in, half, second_in,
    coef, pick, chosen, sending, field, stat_out, stat_in, stat_all,
    local_sem, relay_sem, far_sem, part_send, part_recv, weight_send, weight_recv,
    far_send, far_recv, first_send, first_recv, second_send, second_recv, field_send, field_recv,
    stat_send, stat_recv, node_send, node_recv,
):
    groups, nodes, slots, terms, cells, samples, rows, window = sizes
    edge = side_of(groups)
    depth = nodes // 2
    chunk = terms // (2 * window)
    block = cells // groups
    share = samples // groups
    plan = stage_plan(window)
    stages = len(plan)
    offsets = near_first(window)
    reach = min(2, depth // 2)
    relays = []
    while (reach << len(relays)) * 2 < depth:
        relays.append(reach << len(relays))

    grp = lax.axis_index("grp")
    node = lax.axis_index("node")
    col, row = lax.rem(grp, edge), lax.div(grp, edge)
    level, core = lax.div(node, 2), lax.rem(node, 2)
    twin = level * 2 + (1 - core)

    def place(steps):
        down, along = steps
        return lax.rem(row + down + edge, edge) * edge + lax.rem(col + along + edge, edge)

    def level_peer(step, other=0):
        side = 1 - core if other else core
        return lax.rem(level + step + depth, depth) * 2 + side

    def hops(steps):
        return sum(min(k, edge - k) for k in steps)

    around = sorted(((d, a) for d in range(edge) for a in range(edge) if d or a), key=hops)
    far = edge // 2
    first_steps = [k for k in range(1, edge) if k != far]
    near = sorted({k for k in range(-reach, reach + 1) if k % depth}, key=abs)
    near = [k for i, k in enumerate(near) if k % depth not in [m % depth for m in near[:i]]]
    beside = [k for k in near if abs(k) == 1]

    sent = []

    def send(src, dst, send_sem, recv_sem, to):
        copy = pltpu.make_async_remote_copy(
            src_ref=src, dst_ref=dst, send_sem=send_sem, recv_sem=recv_sem,
            device_id=to, device_id_type=MESH,
        )
        copy.start()
        sent.append(copy)

    def arrived(dst, send_sem, recv_sem):
        pltpu.make_async_remote_copy(
            src_ref=dst, dst_ref=dst, send_sem=send_sem, recv_sem=recv_sem,
            device_id=(grp, twin), device_id_type=MESH,
        ).wait_recv()

    loads = [
        pltpu.make_async_copy(src, dst, local_sem.at[i])
        for i, (src, dst) in enumerate((
            (basis_hbm, basis), (ids_hbm, ids_ref), (counts_hbm, counts_ref), (damage_hbm, damage),
            (table_hbm, table), (new_ids_hbm, new_ids_ref),
        ))
    ]
    loads[0].start()

    barrier = pltpu.get_barrier_semaphore()
    greeted = [(place(steps), node) for steps in reversed(around)]
    greeted += [(grp, level_peer(k)) for k in reversed(near)]
    greeted += [(grp, level_peer(k, 1)) for k in beside] + [(grp, twin)]
    for to in greeted:
        pl.semaphore_signal(barrier, inc=1, device_id=to, device_id_type=MESH)
    for load in loads[1:]:
        load.start()

    index = lax.rem(level, window) * 2 + core
    pick_terms = lax.broadcasted_iota(jnp.int32, (chunk, terms), 1) - index * chunk
    pick_terms = pick_terms == lax.broadcasted_iota(jnp.int32, (chunk, terms), 0)
    pick_terms = jnp.where(pick_terms, 1.0, 0.0).astype(BF16)
    loads[0].wait()
    parts[grp] = lax.dot_general(
        pick_terms, basis[...], (((1,), (1,)), ((), ())), preferred_element_type=F32
    ).astype(BF16)

    pl.semaphore_wait(barrier, len(greeted))

    for steps in reversed(around):
        at = steps[0] * edge + steps[1]
        send(parts.at[grp], parts.at[grp], part_send.at[at], part_recv.at[at], (place(steps), node))
    def far_copies():
        copies = []
        for side, to in ((0, (0, far)), (1, (far, 0))):
            copies.append((ids_ref, far_ids.at[side], side, place(to)))
        across = lax.rem(col + far, edge)
        for q in range(edge):
            columns = pl.ds(pl.multiple_of((q * edge + across) * block, block), block)
            copies.append((damage.at[:, columns], far_damage.at[0, :, q * block : (q + 1) * block], 2 + q, place((0, far))))
        columns = pl.ds(pl.multiple_of(lax.rem(row + far, edge) * edge * block, edge * block), edge * block)
        copies.append((damage.at[:, columns], far_damage.at[1], 2 + edge, place((far, 0))))
        return copies

    loads[1].wait()
    loads[3].wait()
    for src, dst, at, to in far_copies():
        send(src, dst, far_send.at[at], far_recv.at[at], (to, node))

    def relay(i):
        for k in (relays[i], -relays[i]):
            pl.semaphore_signal(relay_sem.at[i], inc=1, device_id=(grp, level_peer(k)), device_id_type=MESH)

    def hear_relay(i):
        pl.semaphore_wait(relay_sem.at[i], 2)
        if i + 1 < len(relays):
            relay(i + 1)

    if relays:
        relay(0)

    loads[2].wait()

    def build(which, ids):
        line = lax.broadcasted_iota(jnp.int32, (slots, slots), 0)
        wanted = jnp.broadcast_to(ids, (slots, slots)) - line

        @pl.loop(0, groups)
        def _(g):
            onehot[which, g] = jnp.where(wanted == g * slots, 1.0, 0.0).astype(BF16)

    build(0, ids_ref[...])

    def choose(part):
        width = samples // edge
        wanted_row = new_ids_ref[:, part * width : (part + 1) * width].astype(F32)
        wanted_row = jnp.broadcast_to(wanted_row, (128, width)).T
        lane = lax.broadcasted_iota(jnp.int32, (width, 128), 1).astype(F32)
        wanted_row = wanted_row - lane
        for q in range(rows // 128):
            pick[:, q * 128 : (q + 1) * 128] = jnp.where(wanted_row == q * 128.0, 1.0, 0.0).astype(BF16)
        chosen[part * width : (part + 1) * width, :] = jnp.dot(
            pick[...], table[...], preferred_element_type=F32
        ).astype(BF16)

    loads[4].wait()
    loads[5].wait()
    for part in range(edge // 2):
        choose(part)
    for _, dst, at, _ in far_copies()[:2]:
        arrived(dst, far_send.at[at], far_recv.at[at])
        build(1 + at, far_ids[at])

    counts = counts_ref[...]
    total = jnp.sum(counts, axis=1, keepdims=True).astype(F32)
    which = lax.broadcasted_iota(jnp.int32, counts.shape, 1)
    owners = (grp, place((0, far)), place((far, 0)))
    live = [jnp.sum(jnp.where(which == owner, counts, 0), axis=1, keepdims=True) for owner in owners]
    mid = chunk // 2

    def rows_from(source):
        return [
            jnp.dot(parts[source], onehot[0, source], preferred_element_type=F32),
            jnp.dot(parts[source, :mid], onehot[1, source], preferred_element_type=F32),
            jnp.dot(parts[source, mid:], onehot[2, source], preferred_element_type=F32),
        ]

    mine = rows_from(grp)
    for steps in around:
        source = place((-steps[0], -steps[1]))
        at = steps[0] * edge + steps[1]
        arrived(parts.at[source], part_send.at[at], part_recv.at[at])
        mine = [have + more for have, more in zip(mine, rows_from(source))]
    slot = lax.broadcasted_iota(jnp.int32, (chunk, slots), 1)
    weights[0, 0] = jnp.where(slot < live[0], mine[0], 0.0).astype(BF16)
    weights[0, 1, :mid] = jnp.where(slot[:mid] < live[1], mine[1], 0.0).astype(BF16)
    weights[0, 1, mid:] = jnp.where(slot[mid:] < live[2], mine[2], 0.0).astype(BF16)

    send(weights.at[0], weights.at[1], weight_send.at[0, 1], weight_recv.at[0, 1], (grp, twin))
    for k in range(1, window):
        if relays and k == 2 * reach + 1:
            hear_relay(0)
        send(
            weights.at[0], weights.at[2 * k], weight_send.at[k, 0], weight_recv.at[k, 0],
            (grp, level_peer(-offsets[k])),
        )
        if abs(offsets[k]) == 1:
            send(
                weights.at[0], weights.at[2 * k + 1], weight_send.at[k, 1], weight_recv.at[k, 1],
                (grp, level_peer(-offsets[k], 1)),
            )

    def pass_on(stage):
        for u in range(*plan[stage]):
            k = u // 2
            if u % 2 == 0 and k:
                arrived(weights.at[2 * k], weight_send.at[k, 0], weight_recv.at[k, 0])
                if abs(offsets[k]) > 1:
                    send(
                        weights.at[2 * k], weights.at[2 * k + 1], weight_send.at[k, 1], weight_recv.at[k, 1],
                        (grp, twin),
                    )

    def lines_of(stage):
        return (plan[stage][1] - plan[stage][0]) * chunk // 2

    def project(stage):
        begin, end = plan[stage]
        lines = lines_of(stage)
        for u in range(begin, end):
            if u % 2:
                arrived(weights.at[u], weight_send.at[u // 2, 1], weight_recv.at[u // 2, 1])
        count = end - begin
        wide = edge * block
        left = weights[begin:end, 0].reshape(2 * lines, slots)
        for r in range(edge):
            product = jnp.dot(left, damage[:, r * wide : (r + 1) * wide], preferred_element_type=F32).astype(BF16)
            product = product.reshape(count, chunk, wide)
            for c in range(edge):
                piece = product[:, :, c * block : (c + 1) * block]
                partial[stage, 0, c, r, :lines] = piece[:, :mid].reshape(lines, block)
                partial[stage, 1, r, c, :lines] = piece[:, mid:].reshape(lines, block)
        for step in first_steps:
            for side, to in ((0, (0, step)), (1, (step, 0))):
                target = lax.rem((row if side else col) + step, edge)
                send(
                    partial.at[stage, side, target, :, :lines], first_in.at[stage, side, step - 1, :, :lines],
                    first_send.at[stage, side, step], first_recv.at[stage, side, step], (place(to), node),
                )

    def add_far(stage):
        begin, end = plan[stage]
        lines = lines_of(stage)
        if stage == 0:
            for _, dst, at, _ in far_copies()[2:]:
                arrived(dst, far_send.at[at], far_recv.at[at])
        for side, own, terms_of in ((0, col, slice(0, mid)), (1, row, slice(mid, chunk))):
            left = weights[begin:end, 1, terms_of].reshape(lines, slots)
            product = jnp.dot(left, far_damage[side], preferred_element_type=F32)
            for q in range(edge):
                amount = partial[stage, side, own, q, :lines].astype(F32) + product[:, q * block : (q + 1) * block]
                partial[stage, side, own, q, :lines] = amount.astype(BF16)

    def middle(stage):
        lines = lines_of(stage)
        add_far(stage)
        for side, own in ((0, col), (1, row)):
            for step in first_steps:
                arrived(
                    first_in.at[stage, side, step - 1, :, :lines],
                    first_send.at[stage, side, step], first_recv.at[stage, side, step],
                )
            for q in range(edge):
                amount = partial[stage, side, own, q, :lines].astype(F32)
                for step in first_steps:
                    amount = amount + first_in[stage, side, step - 1, q, :lines].astype(F32)
                half[stage, side, q, :lines] = amount.astype(BF16)
        for step in sorted(range(1, edge), key=lambda k: -min(k, edge - k)):
            for side, to in ((0, (step, 0)), (1, (0, step))):
                target = lax.rem((col if side else row) + step, edge)
                send(
                    half.at[stage, side, target, :lines], second_in.at[stage, side, step - 1, :lines],
                    second_send.at[stage, side, step], second_recv.at[stage, side, step], (place(to), node),
                )

    def finish(stage):
        lines = lines_of(stage)
        begin, end = plan[stage]
        for side, own in ((0, row), (1, col)):
            for step in range(1, edge):
                arrived(
                    second_in.at[stage, side, step - 1, :lines],
                    second_send.at[stage, side, step], second_recv.at[stage, side, step],
                )
            amount = half[stage, side, own, :lines].astype(F32)
            for step in range(1, edge):
                amount = amount + second_in[stage, side, step - 1, :lines].astype(F32)
            amount = (amount / total).astype(BF16)
            for i in range(end - begin):
                u = begin + i
                owner = lax.rem(level + offsets[u // 2] + depth, window) * 2 + (1 - core if u % 2 else core)
                first = pl.multiple_of(owner * chunk + side * mid, mid)
                coef[pl.ds(first, mid), :] = amount[i * mid : (i + 1) * mid]

    ahead = min(3, stages)
    for stage in range(ahead):
        pass_on(stage)
        project(stage)
    for part in range(edge // 2, edge):
        choose(part)
    for stage in range(stages):
        if stage + ahead < stages:
            pass_on(stage + ahead)
        middle(stage)
        if stage + ahead < stages:
            project(stage + ahead)
        if stage:
            finish(stage - 1)
    for i in range(1 if window > 2 * reach + 1 else 0, len(relays)):
        hear_relay(i)
    pl.semaphore_signal(far_sem, inc=1, device_id=(grp, twin), device_id_type=MESH)
    pl.semaphore_wait(far_sem, 1)
    finish(stages - 1)

    def own_stat(values):
        turned = values.T
        return jnp.sum(turned * turned, axis=0, keepdims=True), jnp.max(turned, axis=0, keepdims=True)

    here = pl.ds(pl.multiple_of(grp * block, block), block)
    wide = edge * share
    order = sorted(range(edge), key=lambda k: -min(k, edge - k))
    for r in order:
        to_row = lax.rem(row + r, edge)
        values = jnp.dot(
            chosen[pl.ds(pl.multiple_of(to_row * wide, wide), wide), :], coef[...], preferred_element_type=F32
        )
        square, largest = own_stat(values)
        stat_out[r, 0:1, :] = square
        stat_out[r, 1:2, :] = largest
        sending[r] = values.astype(BF16).reshape(edge, share, block)
        for c in order:
            if r or c:
                at = r * edge + c
                send(stat_out.at[r], stat_in.at[at], stat_send.at[at], stat_recv.at[at], (place((r, c)), node))
    for r in order:
        for c in order:
            to_col = lax.rem(col + c, edge)
            at = r * edge + c
            if at:
                send(sending.at[r, to_col], field.at[:, here], field_send.at[at], field_recv.at[at], (place((r, c)), node))
    field[:, here] = sending[0, col]

    square, largest = stat_out[0, 0:1, :], stat_out[0, 1:2, :]
    for steps in around:
        at = steps[0] * edge + steps[1]
        arrived(stat_in.at[at], stat_send.at[at], stat_recv.at[at])
        square = square + stat_in[at, 0:1, :]
        largest = jnp.maximum(largest, stat_in[at, 1:2, :])
    stat_all[node, 0:1, :] = square
    stat_all[node, 1:2, :] = largest
    for step in sorted(range(depth), key=lambda k: -min(k, depth - k)):
        for other in (0, 1):
            if step or other:
                at = step * 2 + other
                send(
                    stat_all.at[node], stat_all.at[node], node_send.at[at], node_recv.at[at],
                    (grp, level_peer(step, other)),
                )

    for steps in around:
        at = steps[0] * edge + steps[1]
        source = place((-steps[0], -steps[1]))
        there = pl.ds(pl.multiple_of(source * block, block), block)
        arrived(field.at[:, there], field_send.at[at], field_recv.at[at])
    write = pltpu.make_async_copy(field, out_ref, local_sem.at[len(loads)])
    write.start()

    for step in sorted(range(depth), key=lambda k: min(k, depth - k)):
        for other in (0, 1):
            if step or other:
                at = step * 2 + other
                source = level_peer(-step, other)
                arrived(stat_all.at[source], node_send.at[at], node_recv.at[at])
    square, largest = stat_all[0, 0:1, :], stat_all[0, 1:2, :]
    for k in range(1, nodes):
        square = square + stat_all[k, 0:1, :]
        largest = jnp.maximum(largest, stat_all[k, 1:2, :])
    spread = jnp.sqrt(square / (cells * nodes) + 1e-06)
    result = (largest[:, :share], spread[:, :share])
    for c in range(1, edge):
        mine = slice(c * share, (c + 1) * share)
        result = (jnp.where(col == c, largest[:, mine], result[0]), jnp.where(col == c, spread[:, mine], result[1]))
    stat_ref[0:1, :], stat_ref[1:2, :] = result

    write.wait()
    for copy in sent:
        copy.wait_send()


def local(damage, basis_table, train_ids, counts, new_table, new_ids):
    groups, nodes = lax.axis_size("grp"), lax.axis_size("node")
    slots, cells = damage.shape
    rows, terms = new_table.shape
    samples = new_ids.shape[0]
    edge, depth = side_of(groups), nodes // 2
    window = min(8, depth)
    chunk, block, share = terms // (2 * window), cells // groups, samples // groups
    stages = len(stage_plan(window))
    lines = max(end - begin for begin, end in stage_plan(window)) * chunk // 2
    sizes = (groups, nodes, slots, terms, cells, samples, rows, window)
    dma = pltpu.SemaphoreType.DMA
    hbm = pl.BlockSpec(memory_space=pl.ANY)
    out, stat = pl.pallas_call(
        functools.partial(kernel, sizes),
        out_shape=(
            jax.ShapeDtypeStruct((share, cells), BF16),
            jax.ShapeDtypeStruct((2, share), F32),
        ),
        in_specs=[hbm] * 6,
        out_specs=(pl.BlockSpec(memory_space=pl.ANY), pl.BlockSpec(memory_space=pltpu.VMEM)),
        scratch_shapes=[
            pltpu.VMEM((slots, cells), BF16),
            pltpu.VMEM((2, slots, edge * block), BF16),
            pltpu.VMEM((slots, terms), BF16),
            pltpu.VMEM((1, slots), jnp.int32),
            pltpu.VMEM((2, 1, slots), jnp.int32),
            pltpu.VMEM((1, groups), jnp.int32),
            pltpu.VMEM((rows, terms), BF16),
            pltpu.VMEM((1, samples), jnp.int32),
            pltpu.VMEM((3, groups, slots, slots), BF16),
            pltpu.VMEM((groups, chunk, slots), BF16),
            pltpu.VMEM((2 * window, 2, chunk, slots), BF16),
            pltpu.VMEM((stages, 2, edge, edge, lines, block), BF16),
            pltpu.VMEM((stages, 2, edge - 1, edge, lines, block), BF16),
            pltpu.VMEM((stages, 2, edge, lines, block), BF16),
            pltpu.VMEM((stages, 2, edge - 1, lines, block), BF16),
            pltpu.VMEM((terms, block), BF16),
            pltpu.VMEM((samples // edge, rows), BF16),
            pltpu.VMEM((samples, terms), BF16),
            pltpu.VMEM((edge, edge, share, block), BF16),
            pltpu.VMEM((share, cells), BF16),
            pltpu.VMEM((edge, 2, edge * share), F32),
            pltpu.VMEM((groups, 2, edge * share), F32),
            pltpu.VMEM((nodes, 2, edge * share), F32),
            dma((7,)),
            pltpu.SemaphoreType.REGULAR((4,)),
            pltpu.SemaphoreType.REGULAR,
            dma((groups,)), dma((groups,)),
            dma((window, 2)), dma((window, 2)),
            dma((edge + 3,)), dma((edge + 3,)),
            dma((stages, 2, edge)), dma((stages, 2, edge)),
            dma((stages, 2, edge)), dma((stages, 2, edge)),
            dma((groups,)), dma((groups,)),
            dma((groups,)), dma((groups,)),
            dma((nodes,)), dma((nodes,)),
        ],
        compiler_params=pltpu.CompilerParams(
            collective_id=0, has_side_effects=True, vmem_limit_bytes=61950 * 1024
        ),
        name="projection",
    )(damage, basis_table, train_ids.reshape(1, -1), counts.reshape(1, -1), new_table, new_ids.reshape(1, -1))
    return out, stat[0], stat[1]


def solution(mesh):
    placed = (P("grp", "node"), P("grp", None), P("grp"), P(), P(), P())
    return jax.shard_map(
        local,
        mesh=mesh,
        in_specs=placed,
        out_specs=(P("grp", "node"), P("grp"), P("grp")),
        check_vma=False,
    )
```

```python
import functools

import jax
import jax.numpy as jnp
from jax import lax
from jax.experimental import pallas as pl
from jax.experimental.pallas import tpu as pltpu
from jax.sharding import PartitionSpec as P

MESH = pl.DeviceIdType.MESH
F32 = jnp.float32
BF16 = jnp.bfloat16


def side_of(count):
    side = 1
    while side * side < count:
        side *= 2
    return side


def near_first(count):
    order = [0]
    for step in range(1, count // 2 + 1):
        order += [step, -step]
    return order[:count]


def stage_plan(window):
    cuts = sorted({min(k, 2 * window) for k in (0, 2, 6, 10, 2 * window)})
    return list(zip(cuts[:-1], cuts[1:]))


def kernel(
    sizes,
    damage_hbm, basis_hbm, ids_hbm, counts_hbm, table_hbm, new_ids_hbm,
    out_ref, stat_ref,
    damage, basis, ids_ref, counts_ref, table, new_ids_ref,
    onehot, parts, weights, partial, first_in, half, second_in,
    coef, pick, chosen, sending, field, stat_out, stat_in, stat_all,
    local_sem, relay_sem, far_sem, part_send, part_recv, weight_send, weight_recv,
    first_send, first_recv, second_send, second_recv, field_send, field_recv,
    stat_send, stat_recv, node_send, node_recv,
):
    groups, nodes, slots, terms, cells, samples, rows, window = sizes
    edge = side_of(groups)
    depth = nodes // 2
    chunk = terms // (2 * window)
    block = cells // groups
    share = samples // groups
    plan = stage_plan(window)
    stages = len(plan)
    offsets = near_first(window)
    reach = min(2, depth // 2)
    relays = []
    while (reach << len(relays)) * 2 < depth:
        relays.append(reach << len(relays))

    grp = lax.axis_index("grp")
    node = lax.axis_index("node")
    col, row = lax.rem(grp, edge), lax.div(grp, edge)
    level, core = lax.div(node, 2), lax.rem(node, 2)
    twin = level * 2 + (1 - core)

    def place(steps):
        down, along = steps
        return lax.rem(row + down + edge, edge) * edge + lax.rem(col + along + edge, edge)

    def level_peer(step, other=0):
        side = 1 - core if other else core
        return lax.rem(level + step + depth, depth) * 2 + side

    def hops(steps):
        return sum(min(k, edge - k) for k in steps)

    around = sorted(((d, a) for d in range(edge) for a in range(edge) if d or a), key=hops)
    near = sorted({k for k in range(-reach, reach + 1) if k % depth}, key=abs)
    near = [k for i, k in enumerate(near) if k % depth not in [m % depth for m in near[:i]]]
    beside = [k for k in near if abs(k) == 1]

    sent = []

    def send(src, dst, send_sem, recv_sem, to):
        copy = pltpu.make_async_remote_copy(
            src_ref=src, dst_ref=dst, send_sem=send_sem, recv_sem=recv_sem,
            device_id=to, device_id_type=MESH,
        )
        copy.start()
        sent.append(copy)

    def arrived(dst, send_sem, recv_sem):
        pltpu.make_async_remote_copy(
            src_ref=dst, dst_ref=dst, send_sem=send_sem, recv_sem=recv_sem,
            device_id=(grp, twin), device_id_type=MESH,
        ).wait_recv()

    loads = [
        pltpu.make_async_copy(src, dst, local_sem.at[i])
        for i, (src, dst) in enumerate((
            (basis_hbm, basis), (ids_hbm, ids_ref), (counts_hbm, counts_ref), (damage_hbm, damage),
            (table_hbm, table), (new_ids_hbm, new_ids_ref),
        ))
    ]
    loads[0].start()

    barrier = pltpu.get_barrier_semaphore()
    greeted = [(place(steps), node) for steps in reversed(around)]
    greeted += [(grp, level_peer(k)) for k in reversed(near)]
    greeted += [(grp, level_peer(k, 1)) for k in beside] + [(grp, twin)]
    for to in greeted:
        pl.semaphore_signal(barrier, inc=1, device_id=to, device_id_type=MESH)
    for load in loads[1:]:
        load.start()

    index = lax.rem(level, window) * 2 + core
    pick_terms = lax.broadcasted_iota(jnp.int32, (chunk, terms), 1) - index * chunk
    pick_terms = pick_terms == lax.broadcasted_iota(jnp.int32, (chunk, terms), 0)
    pick_terms = jnp.where(pick_terms, 1.0, 0.0).astype(BF16)
    loads[0].wait()
    parts[grp] = lax.dot_general(
        pick_terms, basis[...], (((1,), (1,)), ((), ())), preferred_element_type=F32
    ).astype(BF16)

    pl.semaphore_wait(barrier, len(greeted))

    for steps in reversed(around):
        at = steps[0] * edge + steps[1]
        send(parts.at[grp], parts.at[grp], part_send.at[at], part_recv.at[at], (place(steps), node))
    def relay(i):
        for k in (relays[i], -relays[i]):
            pl.semaphore_signal(relay_sem.at[i], inc=1, device_id=(grp, level_peer(k)), device_id_type=MESH)

    def hear_relay(i):
        pl.semaphore_wait(relay_sem.at[i], 2)
        if i + 1 < len(relays):
            relay(i + 1)

    if relays:
        relay(0)

    loads[1].wait()
    loads[2].wait()
    line = lax.broadcasted_iota(jnp.int32, (slots, slots), 0)
    wanted = jnp.broadcast_to(ids_ref[...], (slots, slots)) - line

    @pl.loop(0, groups)
    def _(g):
        onehot[g] = jnp.where(wanted == g * slots, 1.0, 0.0).astype(BF16)

    def choose(part):
        width = samples // edge
        wanted_row = new_ids_ref[:, part * width : (part + 1) * width].astype(F32)
        wanted_row = jnp.broadcast_to(wanted_row, (128, width)).T
        lane = lax.broadcasted_iota(jnp.int32, (width, 128), 1).astype(F32)
        wanted_row = wanted_row - lane
        for q in range(rows // 128):
            pick[:, q * 128 : (q + 1) * 128] = jnp.where(wanted_row == q * 128.0, 1.0, 0.0).astype(BF16)
        chosen[part * width : (part + 1) * width, :] = jnp.dot(
            pick[...], table[...], preferred_element_type=F32
        ).astype(BF16)

    loads[4].wait()
    loads[5].wait()
    for part in range(edge):
        choose(part)

    counts = counts_ref[...]
    total = jnp.sum(counts, axis=1, keepdims=True).astype(F32)
    which = lax.broadcasted_iota(jnp.int32, counts.shape, 1)
    live = jnp.sum(jnp.where(which == grp, counts, 0), axis=1, keepdims=True)

    mine = jnp.dot(parts[grp], onehot[grp], preferred_element_type=F32)
    for steps in around:
        source = place((-steps[0], -steps[1]))
        at = steps[0] * edge + steps[1]
        arrived(parts.at[source], part_send.at[at], part_recv.at[at])
        mine = mine + jnp.dot(parts[source], onehot[source], preferred_element_type=F32)
    slot = lax.broadcasted_iota(jnp.int32, (chunk, slots), 1)
    weights[0] = jnp.where(slot < live, mine, 0.0).astype(BF16)

    send(weights.at[0], weights.at[1], weight_send.at[0, 1], weight_recv.at[0, 1], (grp, twin))
    for k in range(1, window):
        if relays and k == 2 * reach + 1:
            hear_relay(0)
        send(
            weights.at[0], weights.at[2 * k], weight_send.at[k, 0], weight_recv.at[k, 0],
            (grp, level_peer(-offsets[k])),
        )
        if abs(offsets[k]) == 1:
            send(
                weights.at[0], weights.at[2 * k + 1], weight_send.at[k, 1], weight_recv.at[k, 1],
                (grp, level_peer(-offsets[k], 1)),
            )

    def pass_on(stage):
        for u in range(*plan[stage]):
            k = u // 2
            if u % 2 == 0 and k:
                arrived(weights.at[2 * k], weight_send.at[k, 0], weight_recv.at[k, 0])
                if abs(offsets[k]) > 1:
                    send(
                        weights.at[2 * k], weights.at[2 * k + 1], weight_send.at[k, 1], weight_recv.at[k, 1],
                        (grp, twin),
                    )

    def lines_of(stage):
        return (plan[stage][1] - plan[stage][0]) * chunk // 2

    def packed(stage, q=None):
        lines = lines_of(stage)
        first = edge * plan[stage][0] * chunk // 2
        if q is None:
            return slice(first, first + edge * lines)
        return slice(first + q * lines, first + (q + 1) * lines)

    def project(stage):
        begin, end = plan[stage]
        lines = lines_of(stage)
        for u in range(begin, end):
            if u % 2:
                arrived(weights.at[u], weight_send.at[u // 2, 1], weight_recv.at[u // 2, 1])
        left = weights[begin:end].reshape(2 * lines, slots)
        for r in range(edge):
            wide = edge * block
            product = jnp.dot(left, damage[:, r * wide : (r + 1) * wide], preferred_element_type=F32).astype(BF16)
            for c in range(edge):
                piece = product[:, c * block : (c + 1) * block]
                partial[0, c, packed(stage, r)] = piece[:lines]
                partial[1, r, packed(stage, c)] = piece[lines:]
        for step in sorted(range(1, edge), key=lambda k: -min(k, edge - k)):
            for side, to in ((0, (0, step)), (1, (step, 0))):
                target = lax.rem((row if side else col) + step, edge)
                send(
                    partial.at[side, target, packed(stage)], first_in.at[side, step - 1, packed(stage)],
                    first_send.at[stage, side, step], first_recv.at[stage, side, step], (place(to), node),
                )

    def middle(stage):
        lines = lines_of(stage)
        for side, own in ((0, col), (1, row)):
            for step in range(1, edge):
                arrived(
                    first_in.at[side, step - 1, packed(stage)],
                    first_send.at[stage, side, step], first_recv.at[stage, side, step],
                )
            for q in range(edge):
                amount = partial[side, own, packed(stage, q)].astype(F32)
                for step in range(1, edge):
                    amount = amount + first_in[side, step - 1, packed(stage, q)].astype(F32)
                half[stage, side, q, :lines] = amount.astype(BF16)
        for step in sorted(range(1, edge), key=lambda k: -min(k, edge - k)):
            for side, to in ((0, (step, 0)), (1, (0, step))):
                target = lax.rem((col if side else row) + step, edge)
                send(
                    half.at[stage, side, target, :lines], second_in.at[stage, side, step - 1, :lines],
                    second_send.at[stage, side, step], second_recv.at[stage, side, step], (place(to), node),
                )

    def finish(stage):
        lines = lines_of(stage)
        begin = plan[stage][0]
        for side, own in ((0, row), (1, col)):
            for step in range(1, edge):
                arrived(
                    second_in.at[stage, side, step - 1, :lines],
                    second_send.at[stage, side, step], second_recv.at[stage, side, step],
                )
            amount = half[stage, side, own, :lines].astype(F32)
            for step in range(1, edge):
                amount = amount + second_in[stage, side, step - 1, :lines].astype(F32)
            amount = (amount / total).astype(BF16)
            piece = min(chunk, lines)
            for i in range(lines // piece):
                at = side * lines + i * piece
                u = begin + at // chunk
                owner = lax.rem(level + offsets[u // 2] + depth, window) * 2 + (1 - core if u % 2 else core)
                first = owner * chunk + at % chunk
                coef[pl.ds(pl.multiple_of(first, piece), piece), :] = amount[i * piece : (i + 1) * piece]

    loads[3].wait()
    ahead = min(3, stages)
    for stage in range(ahead):
        pass_on(stage)
        project(stage)
    for stage in range(stages):
        if stage + ahead < stages:
            pass_on(stage + ahead)
        middle(stage)
        if stage + ahead < stages:
            project(stage + ahead)
        if stage:
            finish(stage - 1)
    for i in range(1 if window > 2 * reach + 1 else 0, len(relays)):
        hear_relay(i)
    pl.semaphore_signal(far_sem, inc=1, device_id=(grp, twin), device_id_type=MESH)
    pl.semaphore_wait(far_sem, 1)
    finish(stages - 1)

    def own_stat(values):
        turned = values.T
        return jnp.sum(turned * turned, axis=0, keepdims=True), jnp.max(turned, axis=0, keepdims=True)

    here = pl.ds(pl.multiple_of(grp * block, block), block)
    wide = edge * share
    order = sorted(range(edge), key=lambda k: -min(k, edge - k))
    for r in order:
        to_row = lax.rem(row + r, edge)
        values = jnp.dot(
            chosen[pl.ds(pl.multiple_of(to_row * wide, wide), wide), :], coef[...], preferred_element_type=F32
        )
        square, largest = own_stat(values)
        stat_out[r, 0:1, :] = square
        stat_out[r, 1:2, :] = largest
        sending[r] = values.astype(BF16).reshape(edge, share, block)
        for c in order:
            if r or c:
                at = r * edge + c
                send(stat_out.at[r], stat_in.at[at], stat_send.at[at], stat_recv.at[at], (place((r, c)), node))
    for r in order:
        for c in order:
            to_col = lax.rem(col + c, edge)
            at = r * edge + c
            if at:
                send(sending.at[r, to_col], field.at[:, here], field_send.at[at], field_recv.at[at], (place((r, c)), node))
    field[:, here] = sending[0, col]

    square, largest = stat_out[0, 0:1, :], stat_out[0, 1:2, :]
    for steps in around:
        at = steps[0] * edge + steps[1]
        arrived(stat_in.at[at], stat_send.at[at], stat_recv.at[at])
        square = square + stat_in[at, 0:1, :]
        largest = jnp.maximum(largest, stat_in[at, 1:2, :])
    stat_all[node, 0:1, :] = square
    stat_all[node, 1:2, :] = largest
    for step in sorted(range(depth), key=lambda k: -min(k, depth - k)):
        for other in (0, 1):
            if step or other:
                at = step * 2 + other
                send(
                    stat_all.at[node], stat_all.at[node], node_send.at[at], node_recv.at[at],
                    (grp, level_peer(step, other)),
                )

    for steps in around:
        at = steps[0] * edge + steps[1]
        source = place((-steps[0], -steps[1]))
        there = pl.ds(pl.multiple_of(source * block, block), block)
        arrived(field.at[:, there], field_send.at[at], field_recv.at[at])
    write = pltpu.make_async_copy(field, out_ref, local_sem.at[len(loads)])
    write.start()

    for step in sorted(range(depth), key=lambda k: min(k, depth - k)):
        for other in (0, 1):
            if step or other:
                at = step * 2 + other
                source = level_peer(-step, other)
                arrived(stat_all.at[source], node_send.at[at], node_recv.at[at])
    square, largest = stat_all[0, 0:1, :], stat_all[0, 1:2, :]
    for k in range(1, nodes):
        square = square + stat_all[k, 0:1, :]
        largest = jnp.maximum(largest, stat_all[k, 1:2, :])
    spread = jnp.sqrt(square / (cells * nodes) + 1e-06)
    result = (largest[:, :share], spread[:, :share])
    for c in range(1, edge):
        mine = slice(c * share, (c + 1) * share)
        result = (jnp.where(col == c, largest[:, mine], result[0]), jnp.where(col == c, spread[:, mine], result[1]))
    stat_ref[0:1, :], stat_ref[1:2, :] = result

    write.wait()
    for copy in sent:
        copy.wait_send()


def local(damage, basis_table, train_ids, counts, new_table, new_ids):
    groups, nodes = lax.axis_size("grp"), lax.axis_size("node")
    slots, cells = damage.shape
    rows, terms = new_table.shape
    samples = new_ids.shape[0]
    edge, depth = side_of(groups), nodes // 2
    window = min(8, depth)
    chunk, block, share = terms // (2 * window), cells // groups, samples // groups
    stages = len(stage_plan(window))
    lines = max(end - begin for begin, end in stage_plan(window)) * chunk // 2
    sizes = (groups, nodes, slots, terms, cells, samples, rows, window)
    dma = pltpu.SemaphoreType.DMA
    hbm = pl.BlockSpec(memory_space=pl.ANY)
    out, stat = pl.pallas_call(
        functools.partial(kernel, sizes),
        out_shape=(
            jax.ShapeDtypeStruct((share, cells), BF16),
            jax.ShapeDtypeStruct((2, share), F32),
        ),
        in_specs=[hbm] * 6,
        out_specs=(pl.BlockSpec(memory_space=pl.ANY), pl.BlockSpec(memory_space=pltpu.VMEM)),
        scratch_shapes=[
            pltpu.VMEM((slots, cells), BF16),
            pltpu.VMEM((slots, terms), BF16),
            pltpu.VMEM((1, slots), jnp.int32),
            pltpu.VMEM((1, groups), jnp.int32),
            pltpu.VMEM((rows, terms), BF16),
            pltpu.VMEM((1, samples), jnp.int32),
            pltpu.VMEM((groups, slots, slots), BF16),
            pltpu.VMEM((groups, chunk, slots), BF16),
            pltpu.VMEM((2 * window, chunk, slots), BF16),
            pltpu.VMEM((2, edge, edge * terms // 2, block), BF16),
            pltpu.VMEM((2, edge - 1, edge * terms // 2, block), BF16),
            pltpu.VMEM((stages, 2, edge, lines, block), BF16),
            pltpu.VMEM((stages, 2, edge - 1, lines, block), BF16),
            pltpu.VMEM((terms, block), BF16),
            pltpu.VMEM((samples // edge, rows), BF16),
            pltpu.VMEM((samples, terms), BF16),
            pltpu.VMEM((edge, edge, share, block), BF16),
            pltpu.VMEM((share, cells), BF16),
            pltpu.VMEM((edge, 2, edge * share), F32),
            pltpu.VMEM((groups, 2, edge * share), F32),
            pltpu.VMEM((nodes, 2, edge * share), F32),
            dma((7,)),
            pltpu.SemaphoreType.REGULAR((4,)),
            pltpu.SemaphoreType.REGULAR,
            dma((groups,)), dma((groups,)),
            dma((window, 2)), dma((window, 2)),
            dma((stages, 2, edge)), dma((stages, 2, edge)),
            dma((stages, 2, edge)), dma((stages, 2, edge)),
            dma((groups,)), dma((groups,)),
            dma((groups,)), dma((groups,)),
            dma((nodes,)), dma((nodes,)),
        ],
        compiler_params=pltpu.CompilerParams(
            collective_id=0, has_side_effects=True, vmem_limit_bytes=61950 * 1024
        ),
        name="projection",
    )(damage, basis_table, train_ids.reshape(1, -1), counts.reshape(1, -1), new_table, new_ids.reshape(1, -1))
    return out, stat[0], stat[1]


def solution(mesh):
    placed = (P("grp", "node"), P("grp", None), P("grp"), P(), P(), P())
    return jax.shard_map(
        local,
        mesh=mesh,
        in_specs=placed,
        out_specs=(P("grp", "node"), P("grp"), P("grp")),
        check_vma=False,
    )
```
